32 devices in a mesh: section: 8 (over z, core), expert: 4 (over y, x).
Axes of the slice: x: 2, y: 2, z: 4, core: 2. Of those that a mesh axis runs over, the one named last changes fastest.
Arguments:
- acts: bfloat16 [8, 512, 2048], P('section', 'expert'), may hold values from -6 to 6
- routes: int32 [8, 512, 2], P('section', 'expert'), may hold values from 0 to 3, all different within a row; in each aligned block of 128 rows (0 to 127, 128 to 255, ..., all dimensions but the last counted through in order) at most 96 rows name the same one
- gates: float32 [8, 512, 2], P('section', 'expert'), may hold values from 0.2 to 1
- norm_gain: float32 [8, 2048], P('section'), may hold values from 0.5 to 1.5
- gate_w: bfloat16 [8, 2048, 4096], P('section', None, 'expert'), may hold values from -0.125 to 0.125
- up_w: bfloat16 [8, 2048, 4096], P('section', None, 'expert'), may hold values from -0.125 to 0.125
- down_w: bfloat16 [8, 4096, 2048], P('section', 'expert'), may hold values from -0.1875 to 0.1875
Outputs:
- result: bfloat16 [8, 512, 2048], P('section', 'expert')
The draws below stay inside these ranges and needn't reach their ends.
Inputs may be any that keep to these rules, and one draw needn't show every extreme that they name: `routes`: each token names 2 different experts. Among the rows of one device, no expert is named by more than 96 tokens, and in every draw some expert is named by exactly 96.
All inputs are finite; a program needn't handle non-finite values.
Results may differ from the reference program's by a relative error of at most 0.005.
Values may be sent and summed in bfloat16 or wider, within the bound.
No kernel may reach another device: no remote copies, remote signals or barrier semaphores. Data moves between devices by JAX's collectives and lax.ppermute only.
A program may use at most 64 MiB of HBM per device.

```python
import math
import jax
import jax.numpy as jnp
import numpy as np
from jax import lax

D = 2048
HID = 1024
NEXP = 4
TOPK = 2
TOK_DEV = 128
CAP = 96
TOK_SECTION = 512
N_SECTION = 8
N_EXPERT = 4


def levels(rng, extent, split, low, top_value):
    loudness, own = 1.0, jax.random.fold_in(rng, 6)
    for axis_at, blocks in split:
        steps = jnp.exp(jax.random.uniform(jax.random.fold_in(own, axis_at), (blocks,), jnp.float32, low / len(split), top_value / len(split)))
        loudness = loudness * jnp.repeat(steps, extent[axis_at] // blocks).reshape([-1 if axis == axis_at else 1 for axis in range(len(extent))])
    return loudness


def assign_block(key, own, number, rows, count, top, most, lean):
    sequence = jax.random.permutation(key, count)
    heavy_load, common = load_shares(count, rows * top, most, lean, True), load_shares(count, rows * top, most, lean, False)
    places = jnp.arange(count)

    def named(lengths, rotation):
        used = int((lengths > 0).sum())
        fixed = max(1, used // 4)
        passed = fixed + (places - fixed + rotation * (used - fixed)) % max(1, count - fixed)
        return jnp.zeros((count,), jnp.int32).at[sequence[jnp.where(places < fixed, places, passed)]].set(jnp.asarray(lengths, jnp.int32))

    lengths = jnp.where(number % 4 == 0, named(heavy_load, number // 4), named(common, number - number // 4 - 1))
    mixed = jax.random.permutation(jax.random.fold_in(own, 3), count)
    giver, sink = mixed[0:count // 2 * 2:2], mixed[1:count // 2 * 2:2]
    room = jnp.minimum(lengths[giver] - 1, most - lengths[sink]) // 2
    room = jnp.where((giver == sequence[0]) | (sink == sequence[0]) | (lengths[sink] == 0), 0, jnp.maximum(room, 0))
    passed = jax.random.randint(jax.random.fold_in(own, 4), (count // 2,), 0, 1 << 20) % (room + 1)
    lengths = lengths.at[giver].add(-passed).at[sink].add(passed)
    items = jnp.searchsorted(jnp.cumsum(lengths), jnp.arange(rows * top), side="right").astype(jnp.int32)
    grid = items.reshape(top, rows).T
    grid = grid[jax.random.permutation(jax.random.fold_in(own, 1), rows)]
    rotation = jax.random.randint(jax.random.fold_in(own, 2), (rows, 1), 0, top)
    return jnp.take_along_axis(grid, (jnp.arange(top)[None, :] + rotation) % top, axis=1)


def load_shares(count, total, most, slope, full):
    portions = [(1 << 20) // math.isqrt(standing ** slope) + 1 for standing in range(1, count + 1)]
    largest = most if full else min(most, max(-(-total // count), total * portions[0] // sum(portions)))
    least = 1 if total - largest >= count - 1 else 0
    given, spare = [largest] + [least] * (count - 1), total - largest - least * (count - 1)
    while spare > 0:
        candidates = [i for i in range(1, count) if given[i] < largest] or [i for i in range(1, count) if given[i] < most]
        mass, left = sum([portions[i] for i in candidates]), spare
        for i in candidates:
            extra = min(most - given[i], max(1, left * portions[i] // mass), spare)
            given[i] = given[i] + extra
            spare = spare - extra
    return np.array(given)


def noise(own_key, shape, scale, reach, cuts=(), kind=jnp.bfloat16):
    array = jax.random.normal(own_key, shape, jnp.float32) * scale
    if len(cuts) > 0:
        array = levels(own_key, shape, cuts, -0.22, 0.18) * array
    return jnp.clip(array, min=-reach, max=reach).astype(kind)


def setup_inputs(seed: int = 0) -> dict:
    splits = jax.random.split(jax.random.key(seed), 8)
    acts = noise(splits[0], (N_SECTION, TOK_SECTION, D), 1.0, 6.0, ((0, 8), (1, 4)))
    routes_keys = jax.random.split(jax.random.fold_in(splits[1], 1), N_SECTION * TOK_SECTION // TOK_DEV)
    routes_turns = jax.random.permutation(jax.random.fold_in(splits[1], 3), N_SECTION * TOK_SECTION // TOK_DEV)
    routes = jax.vmap(lambda own, number: assign_block(jax.random.fold_in(splits[1], 2), own, number, TOK_DEV, NEXP, TOPK, CAP, 2))(routes_keys, routes_turns).reshape((N_SECTION, TOK_SECTION, TOPK))
    gates = jnp.clip(0.2 + 0.8 * jax.random.uniform(splits[2], (N_SECTION, TOK_SECTION, TOPK), jnp.float32) ** levels(splits[2], (N_SECTION, TOK_SECTION, TOPK), ((0, 8), (1, 4)), -0.2, 0.2), 0.2, 1.0)
    norm_gain = jnp.clip(1.0 + 0.1 * jax.random.normal(splits[3], (N_SECTION, D), jnp.float32), 0.5, 1.5)
    gate_w = noise(splits[4], (N_SECTION, D, NEXP * HID), D ** -0.5, 0.125, ((0, 8), (2, 4)))
    up_w = noise(splits[5], (N_SECTION, D, NEXP * HID), D ** -0.5, 0.125, ((0, 8), (2, 4)))
    down_w = noise(splits[6], (N_SECTION, NEXP * HID, D), HID ** -0.5, 0.1875, ((0, 8), (1, 4)))
    return {"acts": acts, "routes": routes, "gates": gates, "norm_gain": norm_gain, "gate_w": gate_w, "up_w": up_w, "down_w": down_w}


def one_section(pack):
    xin, ids, weights, gain, wgate, wup, wdown = pack
    xf = xin.astype(jnp.float32)
    scale = lax.rsqrt(lax.optimization_barrier(jnp.mean(xf * xf, axis=1, keepdims=True)) + 1e-06)
    normed = (xf * scale * gain[None, :]).astype(jnp.bfloat16)
    hsplit = N_EXPERT // NEXP
    width = HID // hsplit
    limit = min(TOK_SECTION, CAP * N_EXPERT)
    total = xf
    for g in range(NEXP):
        chosen = (ids == g).astype(jnp.int32)
        member = lax.optimization_barrier(jnp.sum(chosen, axis=1))
        order = jnp.argsort(1 - member, stable=True)[:limit].astype(jnp.int32)
        rows = normed[order]
        weight_g = lax.optimization_barrier(jnp.sum(weights * chosen.astype(jnp.float32), axis=1))[order]
        expert_out = jnp.zeros((limit, D), jnp.float32)
        for h in range(hsplit):
            first = g * HID + h * width
            gpart = jnp.dot(rows, wgate[:, first:first + width], preferred_element_type=jnp.float32)
            upart = jnp.dot(rows, wup[:, first:first + width], preferred_element_type=jnp.float32)
            hidden = (jax.nn.silu(gpart) * upart).astype(jnp.bfloat16)
            part = jnp.dot(hidden, wdown[first:first + width, :], preferred_element_type=jnp.float32).astype(jnp.bfloat16)
            expert_out = expert_out + part.astype(jnp.float32)
        total = total.at[order].add(weight_g[:, None] * expert_out)
    return total.astype(jnp.bfloat16)

def reference(acts, routes, gates, norm_gain, gate_w, up_w, down_w):
    incoming = jnp.roll(acts, 1, axis=0)
    return lax.map(one_section, (incoming, routes, gates, norm_gain, gate_w, up_w, down_w))
```

```python
import functools

import jax
import jax.numpy as jnp
from jax import lax
from jax.experimental import pallas as pl
from jax.experimental.pallas import tpu as pltpu
from jax.sharding import PartitionSpec as P

NEXP = 4
CAP = 96
VMEM = pltpu.VMEM
SMEM = pltpu.SMEM


def shifted(value, axis, steps):
    count = lax.axis_size(axis)
    pairs = [(source, (source + steps) % count) for source in range(count)]
    return lax.ppermute(value, axis, pairs)


def expert_rows(rows, wgate, wup, wdown):
    gpart = jnp.einsum("scd,dh->sch", rows, wgate, preferred_element_type=jnp.float32)
    upart = jnp.einsum("scd,dh->sch", rows, wup, preferred_element_type=jnp.float32)
    hidden = (jax.nn.silu(gpart) * upart).astype(jnp.bfloat16)
    return jnp.einsum("sch,hd->scd", hidden, wdown, preferred_element_type=jnp.float32).astype(
        jnp.bfloat16
    )


def local_any(acts, routes, gates, norm_gain, gate_w, up_w, down_w):
    arrived = shifted(acts, "section", 1)[0]
    ids = routes[0]
    weights = gates[0]
    gain = norm_gain[0]
    wgate = gate_w[0]
    wup = up_w[0]
    wdown = down_w[0]
    hsplit = lax.axis_size("expert") // NEXP
    tok_count = ids.shape[0]
    chosen = (ids[:, :, None] == jnp.arange(NEXP, dtype=jnp.int32)[None, None, :]).astype(jnp.int32)
    member = jnp.sum(chosen, axis=1)
    gate_of = jnp.sum(weights[:, :, None] * chosen.astype(jnp.float32), axis=1)
    slot_rank = jnp.cumsum(member, axis=0) - 1
    slots = jnp.arange(CAP, dtype=jnp.int32)
    place = (slot_rank.T[:, None, :] == slots[None, :, None]) & (member.T[:, None, :] > 0)
    place_bf = place.astype(jnp.bfloat16)
    xf = arrived.astype(jnp.float32)
    scale = lax.rsqrt(jnp.mean(xf * xf, axis=1, keepdims=True) + 1e-06)
    normed = (xf * scale * gain[None, :]).astype(jnp.bfloat16)
    packed = jnp.einsum("gct,td->gcd", place_bf, normed, preferred_element_type=jnp.float32).astype(
        jnp.bfloat16
    )
    outgoing = jnp.repeat(packed, hsplit, axis=0)
    received = lax.all_to_all(outgoing, "expert", split_axis=0, concat_axis=0, tiled=True)
    returned = lax.all_to_all(
        expert_rows(received, wgate, wup, wdown), "expert", split_axis=0, concat_axis=0, tiled=True
    )
    shards = returned.reshape(NEXP, hsplit, CAP, returned.shape[-1])
    per_expert = jnp.einsum("gct,ghcd->gtd", place_bf, shards, preferred_element_type=jnp.float32)
    contrib = jnp.sum(per_expert * gate_of.T[:, :, None], axis=0)
    result = (xf + contrib).astype(jnp.bfloat16)
    return result.reshape(1, tok_count, result.shape[-1])


def spec(space=VMEM):
    return pl.BlockSpec(memory_space=space)


def call(body, outs, ins, spaces, limit=16, flops=0, scratch=()):
    moved = sum(v.size * v.dtype.itemsize for v in (*ins, *outs))
    return pl.pallas_call(
        body,
        out_shape=outs,
        in_specs=[spec(s) for s in spaces],
        out_specs=[spec() for _ in outs],
        scratch_shapes=scratch,
        compiler_params=pltpu.CompilerParams(vmem_limit_bytes=limit << 20),
        cost_estimate=pl.CostEstimate(flops=flops, bytes_accessed=moved, transcendentals=0),
    )(*ins)


def like(shape, dtype=jnp.bfloat16):
    return jax.ShapeDtypeStruct(shape, dtype)


def members(ids, who, count):
    rows = [((ids[0:1, :] == who[k]) | (ids[1:2, :] == who[k])).astype(jnp.float32) for k in range(count)]
    rows += [jnp.zeros_like(rows[0])] * (8 - count)
    return jnp.concatenate(rows, axis=0)


def ranks(member):
    tokens = member.shape[1]
    before = lax.broadcasted_iota(jnp.int32, (tokens, tokens), 0)
    at = lax.broadcasted_iota(jnp.int32, (tokens, tokens), 1)
    upto = (before <= at).astype(jnp.bfloat16)
    return jnp.dot(member.astype(jnp.bfloat16), upto, preferred_element_type=jnp.float32) - 1.0


def one_hot(member, rank, k):
    slots = lax.broadcasted_iota(jnp.int32, (CAP, member.shape[1]), 0).astype(jnp.float32)
    hit = (slots == rank[k : k + 1, :]) & (member[k : k + 1, :] > 0)
    return hit.astype(jnp.bfloat16)


def pack_body(count, who, ids, rows, gain, *outs):
    xf = rows[...].astype(jnp.float32)
    scale = lax.rsqrt(jnp.mean(xf * xf, axis=1, keepdims=True) + 1e-06)
    normed = (xf * scale * gain[...]).astype(jnp.bfloat16)
    member = members(ids[...], who, count)
    rank = ranks(member)
    for k in range(count):
        place = one_hot(member, rank, k)
        outs[k][...] = jnp.dot(place, normed, preferred_element_type=jnp.float32).astype(jnp.bfloat16)


def pack(who, ids, rows, gain, count):
    out = like((CAP, rows.shape[1]))
    return call(
        functools.partial(pack_body, count), [out] * count, (who, ids, rows, gain), (SMEM, VMEM, VMEM, VMEM)
    )


def ffn_body(count, *refs):
    xs, (wgate, wup, wdown), outs = refs[:count], refs[count : count + 3], refs[count + 3 :]
    x = xs[0][...] if count == 1 else jnp.concatenate([r[...] for r in xs], axis=0)
    gpart = jnp.dot(x, wgate[...], preferred_element_type=jnp.float32)
    upart = jnp.dot(x, wup[...], preferred_element_type=jnp.float32)
    hidden = (gpart * jax.nn.sigmoid(gpart) * upart).astype(jnp.bfloat16)
    part = jnp.dot(hidden, wdown[...], preferred_element_type=jnp.float32).astype(jnp.bfloat16)
    for k in range(count):
        outs[k][...] = part[k * CAP : (k + 1) * CAP]


def ffn(xs, weights):
    count = len(xs)
    flops = 6 * count * CAP * weights[0].size
    return call(
        functools.partial(ffn_body, count),
        [like((CAP, weights[2].shape[1]))] * count,
        (*xs, *weights),
        [VMEM] * (count + 3),
        limit=32,
        flops=flops,
    )


def combine_body(count, who, ids, gates, rows, *refs):
    parts, out = refs[:count], refs[count]
    member = members(ids[...], who, count)
    rank = ranks(member)
    weight = [
        jnp.where(ids[0:1, :] == who[k], gates[0:1, :], 0.0) + jnp.where(ids[1:2, :] == who[k], gates[1:2, :], 0.0)
        for k in range(count)
    ]
    weight = jnp.concatenate(weight + [jnp.zeros_like(weight[0])] * (8 - count), axis=0).T
    total = rows[...].astype(jnp.float32)
    for k in range(count):
        place = one_hot(member, rank, k)
        spread = lax.dot_general(
            place, parts[k][...], (((0,), (0,)), ((), ())), preferred_element_type=jnp.float32
        )
        total = total + weight[:, k : k + 1] * spread
    out[...] = total.astype(jnp.bfloat16)


def combine(who, ids, gates, rows, parts):
    count = len(parts)
    return call(
        functools.partial(combine_body, count),
        [like(rows.shape)],
        (who, ids, gates, rows, *parts),
        [SMEM] + [VMEM] * (count + 3),
    )[0]


def swapped(value, flip):
    return lax.ppermute(value, "expert", [(e, e ^ flip) for e in range(NEXP)])


def local_square(acts, routes, gates, norm_gain, gate_w, up_w, down_w):
    arrived = shifted(acts, "section", 1)[0]
    me = lax.axis_index("expert").astype(jnp.int32)
    who = jnp.stack([me, me ^ 1, me ^ 2, me ^ 3])
    ids = routes[0].T
    weights = (gate_w[0], up_w[0], down_w[0])
    own, px, py, pd = pack(who, ids, arrived, norm_gain, NEXP)
    pd = swapped(pd, 3)
    px = swapped(px, 1)
    py = swapped(py, 2)
    (td,) = ffn([pd], weights)
    td = swapped(td, 3)
    tx, ty = ffn([px, py], weights)
    tx = swapped(tx, 1)
    ty = swapped(ty, 2)
    (to,) = ffn([own], weights)
    result = combine(who, ids, gates[0].T, arrived, [to, tx, ty, td])
    return result[None]


def solution(mesh):
    in_specs = (
        P("section", "expert", None),
        P("section", "expert", None),
        P("section", "expert", None),
        P("section", None),
        P("section", None, "expert"),
        P("section", None, "expert"),
        P("section", "expert", None),
    )
    out_specs = P("section", "expert", None)
    local = local_square if mesh.shape["expert"] == NEXP else local_any
    return jax.shard_map(local, mesh=mesh, in_specs=in_specs, out_specs=out_specs, check_vma=False)
```

```python
import functools

import jax
import jax.numpy as jnp
from jax import lax
from jax.experimental import pallas as pl
from jax.experimental.pallas import tpu as pltpu
from jax.sharding import PartitionSpec as P

NEXP = 4
CAP = 96
VMEM = pltpu.VMEM


def shifted(value, axis, steps):
    count = lax.axis_size(axis)
    pairs = [(source, (source + steps) % count) for source in range(count)]
    return lax.ppermute(value, axis, pairs)


def expert_rows(rows, wgate, wup, wdown):
    gpart = jnp.einsum("scd,dh->sch", rows, wgate, preferred_element_type=jnp.float32)
    upart = jnp.einsum("scd,dh->sch", rows, wup, preferred_element_type=jnp.float32)
    hidden = (jax.nn.silu(gpart) * upart).astype(jnp.bfloat16)
    return jnp.einsum("sch,hd->scd", hidden, wdown, preferred_element_type=jnp.float32).astype(
        jnp.bfloat16
    )


def local_any(acts, routes, gates, norm_gain, gate_w, up_w, down_w):
    arrived = shifted(acts, "section", 1)[0]
    ids = routes[0]
    weights = gates[0]
    gain = norm_gain[0]
    wgate = gate_w[0]
    wup = up_w[0]
    wdown = down_w[0]
    hsplit = lax.axis_size("expert") // NEXP
    tok_count = ids.shape[0]
    chosen = (ids[:, :, None] == jnp.arange(NEXP, dtype=jnp.int32)[None, None, :]).astype(jnp.int32)
    member = jnp.sum(chosen, axis=1)
    gate_of = jnp.sum(weights[:, :, None] * chosen.astype(jnp.float32), axis=1)
    slot_rank = jnp.cumsum(member, axis=0) - 1
    slots = jnp.arange(CAP, dtype=jnp.int32)
    place = (slot_rank.T[:, None, :] == slots[None, :, None]) & (member.T[:, None, :] > 0)
    place_bf = place.astype(jnp.bfloat16)
    xf = arrived.astype(jnp.float32)
    scale = lax.rsqrt(jnp.mean(xf * xf, axis=1, keepdims=True) + 1e-06)
    normed = (xf * scale * gain[None, :]).astype(jnp.bfloat16)
    packed = jnp.einsum("gct,td->gcd", place_bf, normed, preferred_element_type=jnp.float32).astype(
        jnp.bfloat16
    )
    outgoing = jnp.repeat(packed, hsplit, axis=0)
    received = lax.all_to_all(outgoing, "expert", split_axis=0, concat_axis=0, tiled=True)
    returned = lax.all_to_all(
        expert_rows(received, wgate, wup, wdown), "expert", split_axis=0, concat_axis=0, tiled=True
    )
    shards = returned.reshape(NEXP, hsplit, CAP, returned.shape[-1])
    per_expert = jnp.einsum("gct,ghcd->gtd", place_bf, shards, preferred_element_type=jnp.float32)
    contrib = jnp.sum(per_expert * gate_of.T[:, :, None], axis=0)
    result = (xf + contrib).astype(jnp.bfloat16)
    return result.reshape(1, tok_count, result.shape[-1])


def spec(space=VMEM):
    return pl.BlockSpec(memory_space=space)


def call(body, outs, ins, limit=16, flops=0, scratch=()):
    return pl.pallas_call(
        body,
        out_shape=outs,
        in_specs=[spec()] * len(ins),
        out_specs=[spec() for _ in outs],
        scratch_shapes=scratch,
        compiler_params=pltpu.CompilerParams(vmem_limit_bytes=limit << 20),
        cost_estimate=pl.CostEstimate(flops=flops, bytes_accessed=0, transcendentals=0),
    )(*ins)


def like(shape, dtype=jnp.bfloat16):
    return jax.ShapeDtypeStruct(shape, dtype)


def flips(section):
    odd = section % 2
    return 1 + odd, 2 - odd


def position():
    me = lax.axis_index("expert")
    return me, me ^ (2 - lax.rem(lax.axis_index("section"), 2))


def table_body(ids, gates, gain, table, gain_out, ids_here, gates_here, done):
    copies = [(ids, ids_here), (gates, gates_here), (gain, gain_out)]
    copies = [pltpu.make_async_copy(source, target, done.at[n]) for n, (source, target) in enumerate(copies)]
    for copy in copies:
        copy.start()
    for copy in copies:
        copy.wait()
    table[0:2, :] = ids_here[...].astype(jnp.float32)
    table[2:4, :] = gates_here[...]
    table[4:8, :] = jnp.zeros((4, table.shape[1]), jnp.float32)


def tabled(ids, gates, gain):
    ins = [pltpu.with_memory_space_constraint(v, pltpu.HBM) for v in (ids, gates, gain)]
    return pl.pallas_call(
        table_body,
        out_shape=[like((8, ids.shape[1]), jnp.float32), like(gain.shape, gain.dtype)],
        in_specs=[spec(pltpu.HBM)] * 3,
        out_specs=[spec()] * 2,
        scratch_shapes=[VMEM(ids.shape, ids.dtype), VMEM(gates.shape, gates.dtype), pltpu.SemaphoreType.DMA((3,))],
        compiler_params=pltpu.CompilerParams(vmem_limit_bytes=4 << 20),
        cost_estimate=pl.CostEstimate(flops=LONG, bytes_accessed=0, transcendentals=0),
    )(*ins)


OWN_HERE, OWN_SIDE, NEAR_HERE, NEAR_SIDE = range(4)


def routing_body(own, near, place, place_t, weight_t):
    me, side = position()
    ask = [(own, me), (own, side), (near, me), (near, side)]
    names = [(table[0:1, :] == g.astype(jnp.float32), table[1:2, :] == g.astype(jnp.float32)) for table, g in ask]
    rows = [(first | second).astype(jnp.float32) for first, second in names]
    member = jnp.concatenate(rows + [jnp.zeros_like(rows[0])] * (8 - len(rows)), axis=0)
    tokens = member.shape[1]
    before = lax.broadcasted_iota(jnp.int32, (tokens, tokens), 0)
    at = lax.broadcasted_iota(jnp.int32, (tokens, tokens), 1)
    upto = (before <= at).astype(jnp.bfloat16)
    rank = jnp.dot(member.astype(jnp.bfloat16), upto, preferred_element_type=jnp.float32) - 1.0
    slots = lax.broadcasted_iota(jnp.int32, (CAP, tokens), 0).astype(jnp.float32)
    lanes = lax.broadcasted_iota(jnp.int32, (tokens, CAP), 1).astype(jnp.float32)
    member_t, rank_t = member.T, rank.T
    for k in range(len(ask)):
        hit = (slots == rank[k : k + 1, :]) & (member[k : k + 1, :] > 0)
        place[k * CAP : (k + 1) * CAP, :] = hit.astype(jnp.bfloat16)
        hit = (lanes == rank_t[:, k : k + 1]) & (member_t[:, k : k + 1] > 0)
        place_t[k * tokens : (k + 1) * tokens, :] = hit.astype(jnp.bfloat16)
    weight = [
        jnp.where(first, table[2:3, :], 0.0) + jnp.where(second, table[3:4, :], 0.0)
        for (table, _), (first, second) in zip(ask, names)
    ]
    weight_t[...] = jnp.concatenate(weight + [jnp.zeros_like(weight[0])] * (8 - len(weight)), axis=0).T


def routing(own, near):
    tokens = own.shape[1]
    outs = [like((4 * CAP, tokens)), like((4 * tokens, CAP)), like((tokens, 8), jnp.float32)]
    return call(routing_body, outs, (own, near))


def packed(place, k, rows):
    hit = place[k * CAP : (k + 1) * CAP, :]
    return jnp.dot(hit, rows[...], preferred_element_type=jnp.float32).astype(jnp.bfloat16)


def pack_body(k, rows, place, after, out):
    out[...] = packed(place, k, rows)


def pack(k, rows, place, after):
    return call(functools.partial(pack_body, k), [like((CAP, rows.shape[1]))], (rows, place, after))[0]


def expert(rows, gain, wgate, wup, wdown):
    xf = rows.astype(jnp.float32)
    scale = lax.rsqrt(jnp.mean(xf * xf, axis=1, keepdims=True) + 1e-06)
    x = (xf * scale * gain[...]).astype(jnp.bfloat16)
    gpart = jnp.dot(x, wgate[...], preferred_element_type=jnp.float32)
    upart = jnp.dot(x, wup[...], preferred_element_type=jnp.float32)
    hidden = (gpart * jax.nn.sigmoid(gpart) * upart).astype(jnp.bfloat16)
    return jnp.dot(hidden, wdown[...], preferred_element_type=jnp.float32).astype(jnp.bfloat16)


def slots_body(rows, gain, wgate, wup, wdown, after, out):
    out[...] = expert(rows[...], gain, wgate, wup, wdown)


def slots(rows, gain, weights, after):
    outs = [like((CAP, weights[2].shape[1]))]
    return call(slots_body, outs, (rows, gain, *weights, after), flops=6 * CAP * weights[0].size)[0]


def tokens_body(k, rows, place, gain, wgate, wup, wdown, after, out):
    out[...] = expert(packed(place, k, rows), gain, wgate, wup, wdown)


def tokens(k, rows, place, gain, weights, after):
    outs = [like((CAP, weights[2].shape[1]))]
    ins = (rows, place, gain, *weights, after)
    return call(functools.partial(tokens_body, k), outs, ins, flops=6 * CAP * weights[0].size)[0]


STRIP = 256


def spread_body(which, count, *refs):
    bases, (place_t, weight_t, *parts), out = refs[:count], refs[count:-2], refs[-1]
    size = weight_t.shape[0]
    for at in range(0, out.shape[1], STRIP):
        strip = slice(at, at + STRIP)
        terms = [base[:, strip].astype(jnp.float32) for base in bases]
        for k, part in zip(which, parts):
            hit = place_t[k * size : (k + 1) * size, :]
            terms.append(weight_t[:, k : k + 1] * jnp.dot(hit, part[:, strip], preferred_element_type=jnp.float32))
        out[:, strip] = sum(terms[1:], terms[0]).astype(out.dtype)


def spread(which, bases, place_t, weight_t, parts, dtype, after):
    outs = [like((weight_t.shape[0], parts[0].shape[1]), dtype)]
    body = functools.partial(spread_body, which, len(bases))
    return call(body, outs, (*bases, place_t, weight_t, *parts, after))[0]


def added_body(left, right, out):
    for at in range(0, out.shape[1], STRIP):
        strip = slice(at, at + STRIP)
        out[:, strip] = (left[:, strip] + right[:, strip].astype(jnp.float32)).astype(out.dtype)


def moved(value, back, flip):
    sections, experts = lax.axis_size("section"), lax.axis_size("expert")
    pairs = [
        ((s - back) % sections * experts + (e ^ flip(s)), s * experts + e)
        for s in range(sections)
        for e in range(experts)
    ]
    return lax.ppermute(value, ("section", "expert"), pairs)


def near_flip(section):
    return flips(section)[0]


def side_flip(section):
    return flips(section)[1]


LONG = 20_000_000_000


def local_square(acts, routes, gates, norm_gain, gate_w, up_w, down_w):
    weights = (gate_w[0], up_w[0], down_w[0])
    near_rows = moved(acts[0], 1, near_flip)
    table, gain = tabled(routes[0].T, gates[0].T, norm_gain)
    near_table = moved(table, 0, near_flip)
    rows = moved(acts[0], 1, lambda s: 0)
    place, place_t, weight_t = routing(table, near_table)
    onward = pack(NEAR_SIDE, near_rows, place, near_rows)
    far_rows = moved(onward, 0, side_flip)
    near_out = tokens(NEAR_HERE, near_rows, place, gain, weights, onward)
    side_send = pack(OWN_SIDE, rows, place, near_out)
    side_rows = moved(side_send, 0, side_flip)
    far_out = slots(far_rows, gain, weights, side_send)
    on_out = moved(far_out, 0, side_flip)
    side_out = slots(side_rows, gain, weights, far_out)
    from_side = moved(side_out, 0, side_flip)
    back = spread((NEAR_HERE, NEAR_SIDE), (), place_t, weight_t, (near_out, on_out), jnp.bfloat16, side_out)
    from_near = moved(back, 0, near_flip)
    here = tokens(OWN_HERE, rows, place, gain, weights, back)
    total = spread((OWN_HERE, OWN_SIDE), (rows,), place_t, weight_t, (here, from_side), jnp.float32, here)
    return call(added_body, [like(total.shape)], (total, from_near))[0][None]


def solution(mesh):
    in_specs = (
        P("section", "expert", None),
        P("section", "expert", None),
        P("section", "expert", None),
        P("section", None),
        P("section", None, "expert"),
        P("section", None, "expert"),
        P("section", "expert", None),
    )
    out_specs = P("section", "expert", None)
    local = local_square if mesh.shape["expert"] == NEXP else local_any
    return jax.shard_map(local, mesh=mesh, in_specs=in_specs, out_specs=out_specs, check_vma=False)
```

```python
import functools

import jax
import jax.numpy as jnp
from jax import lax
from jax.experimental import pallas as pl
from jax.experimental.pallas import tpu as pltpu
from jax.sharding import PartitionSpec as P

NEXP = 4
CAP = 96
VMEM = pltpu.VMEM


def shifted(value, axis, steps):
    count = lax.axis_size(axis)
    pairs = [(source, (source + steps) % count) for source in range(count)]
    return lax.ppermute(value, axis, pairs)


def expert_rows(rows, wgate, wup, wdown):
    gpart = jnp.einsum("scd,dh->sch", rows, wgate, preferred_element_type=jnp.float32)
    upart = jnp.einsum("scd,dh->sch", rows, wup, preferred_element_type=jnp.float32)
    hidden = (jax.nn.silu(gpart) * upart).astype(jnp.bfloat16)
    return jnp.einsum("sch,hd->scd", hidden, wdown, preferred_element_type=jnp.float32).astype(
        jnp.bfloat16
    )


def local_any(acts, routes, gates, norm_gain, gate_w, up_w, down_w):
    arrived = shifted(acts, "section", 1)[0]
    ids = routes[0]
    weights = gates[0]
    gain = norm_gain[0]
    wgate = gate_w[0]
    wup = up_w[0]
    wdown = down_w[0]
    hsplit = lax.axis_size("expert") // NEXP
    tok_count = ids.shape[0]
    chosen = (ids[:, :, None] == jnp.arange(NEXP, dtype=jnp.int32)[None, None, :]).astype(jnp.int32)
    member = jnp.sum(chosen, axis=1)
    gate_of = jnp.sum(weights[:, :, None] * chosen.astype(jnp.float32), axis=1)
    slot_rank = jnp.cumsum(member, axis=0) - 1
    slots = jnp.arange(CAP, dtype=jnp.int32)
    place = (slot_rank.T[:, None, :] == slots[None, :, None]) & (member.T[:, None, :] > 0)
    place_bf = place.astype(jnp.bfloat16)
    xf = arrived.astype(jnp.float32)
    scale = lax.rsqrt(jnp.mean(xf * xf, axis=1, keepdims=True) + 1e-06)
    normed = (xf * scale * gain[None, :]).astype(jnp.bfloat16)
    packed = jnp.einsum("gct,td->gcd", place_bf, normed, preferred_element_type=jnp.float32).astype(
        jnp.bfloat16
    )
    outgoing = jnp.repeat(packed, hsplit, axis=0)
    received = lax.all_to_all(outgoing, "expert", split_axis=0, concat_axis=0, tiled=True)
    returned = lax.all_to_all(
        expert_rows(received, wgate, wup, wdown), "expert", split_axis=0, concat_axis=0, tiled=True
    )
    shards = returned.reshape(NEXP, hsplit, CAP, returned.shape[-1])
    per_expert = jnp.einsum("gct,ghcd->gtd", place_bf, shards, preferred_element_type=jnp.float32)
    contrib = jnp.sum(per_expert * gate_of.T[:, :, None], axis=0)
    result = (xf + contrib).astype(jnp.bfloat16)
    return result.reshape(1, tok_count, result.shape[-1])


def spec(space=VMEM):
    return pl.BlockSpec(memory_space=space)


def call(body, outs, ins, limit=16, flops=0, scratch=()):
    return pl.pallas_call(
        body,
        out_shape=outs,
        in_specs=[spec()] * len(ins),
        out_specs=[spec() for _ in outs],
        scratch_shapes=scratch,
        compiler_params=pltpu.CompilerParams(vmem_limit_bytes=limit << 20),
        cost_estimate=pl.CostEstimate(flops=flops, bytes_accessed=0, transcendentals=0),
    )(*ins)


def like(shape, dtype=jnp.bfloat16):
    return jax.ShapeDtypeStruct(shape, dtype)


def flips(section):
    odd = section % 2
    return 1 + odd, 2 - odd


def position():
    me = lax.axis_index("expert")
    return me, me ^ (2 - lax.rem(lax.axis_index("section"), 2))


def table_body(ids, gates, gain, table, gain_out, ids_here, gates_here, done):
    copies = [(ids, ids_here), (gates, gates_here), (gain, gain_out)]
    copies = [pltpu.make_async_copy(source, target, done.at[n]) for n, (source, target) in enumerate(copies)]
    for copy in copies:
        copy.start()
    for copy in copies:
        copy.wait()
    table[0:2, :] = ids_here[...].astype(jnp.float32)
    table[2:4, :] = gates_here[...]
    table[4:8, :] = jnp.zeros((4, table.shape[1]), jnp.float32)


def tabled(ids, gates, gain):
    ins = [pltpu.with_memory_space_constraint(v, pltpu.HBM) for v in (ids, gates, gain)]
    return pl.pallas_call(
        table_body,
        out_shape=[like((8, ids.shape[1]), jnp.float32), like(gain.shape, gain.dtype)],
        in_specs=[spec(pltpu.HBM)] * 3,
        out_specs=[spec()] * 2,
        scratch_shapes=[VMEM(ids.shape, ids.dtype), VMEM(gates.shape, gates.dtype), pltpu.SemaphoreType.DMA((3,))],
        compiler_params=pltpu.CompilerParams(vmem_limit_bytes=4 << 20),
        cost_estimate=pl.CostEstimate(flops=LONG, bytes_accessed=0, transcendentals=0),
    )(*ins)


OWN_HERE, OWN_SIDE, NEAR_HERE, NEAR_SIDE = range(4)


def routing_body(own, near, sent, place, place_t, weight_t, rows, done):
    copy = pltpu.make_async_copy(sent, rows, done)
    copy.start()
    me, side = position()
    ask = [(own, me), (own, side), (near, me), (near, side)]
    names = [(table[0:1, :] == g.astype(jnp.float32), table[1:2, :] == g.astype(jnp.float32)) for table, g in ask]
    rows = [(first | second).astype(jnp.float32) for first, second in names]
    member = jnp.concatenate(rows + [jnp.zeros_like(rows[0])] * (8 - len(rows)), axis=0)
    tokens = member.shape[1]
    before = lax.broadcasted_iota(jnp.int32, (tokens, tokens), 0)
    at = lax.broadcasted_iota(jnp.int32, (tokens, tokens), 1)
    upto = (before <= at).astype(jnp.bfloat16)
    rank = jnp.dot(member.astype(jnp.bfloat16), upto, preferred_element_type=jnp.float32) - 1.0
    slots = lax.broadcasted_iota(jnp.int32, (CAP, tokens), 0).astype(jnp.float32)
    lanes = lax.broadcasted_iota(jnp.int32, (tokens, CAP), 1).astype(jnp.float32)
    member_t, rank_t = member.T, rank.T
    for k in range(len(ask)):
        hit = (slots == rank[k : k + 1, :]) & (member[k : k + 1, :] > 0)
        place[k * CAP : (k + 1) * CAP, :] = hit.astype(jnp.bfloat16)
        hit = (lanes == rank_t[:, k : k + 1]) & (member_t[:, k : k + 1] > 0)
        place_t[k * tokens : (k + 1) * tokens, :] = hit.astype(jnp.bfloat16)
    weight = [
        jnp.where(first, table[2:3, :], 0.0) + jnp.where(second, table[3:4, :], 0.0)
        for (table, _), (first, second) in zip(ask, names)
    ]
    weight_t[...] = jnp.concatenate(weight + [jnp.zeros_like(weight[0])] * (8 - len(weight)), axis=0).T
    copy.wait()


def routing(own, near, sent):
    tokens = own.shape[1]
    outs = [like((4 * CAP, tokens)), like((4 * tokens, CAP)), like((tokens, 8), jnp.float32), like(sent.shape)]
    return pl.pallas_call(
        routing_body,
        out_shape=outs,
        in_specs=[spec()] * 2 + [spec(pltpu.HBM)],
        out_specs=[spec()] * 4,
        scratch_shapes=[pltpu.SemaphoreType.DMA],
        compiler_params=pltpu.CompilerParams(vmem_limit_bytes=8 << 20),
        cost_estimate=pl.CostEstimate(flops=0, bytes_accessed=0, transcendentals=0),
    )(own, near, pltpu.with_memory_space_constraint(sent, pltpu.HBM))


def packed(place, k, rows):
    hit = place[k * CAP : (k + 1) * CAP, :]
    return jnp.dot(hit, rows[...], preferred_element_type=jnp.float32).astype(jnp.bfloat16)


def pack_body(k, rows, place, after, out):
    out[...] = packed(place, k, rows)


def pack(k, rows, place, after):
    return call(functools.partial(pack_body, k), [like((CAP, rows.shape[1]))], (rows, place, after))[0]


def expert(rows, gain, wgate, wup, wdown):
    xf = rows.astype(jnp.float32)
    scale = lax.rsqrt(jnp.mean(xf * xf, axis=1, keepdims=True) + 1e-06)
    x = (xf * scale * gain[...]).astype(jnp.bfloat16)
    gpart = jnp.dot(x, wgate[...], preferred_element_type=jnp.float32)
    upart = jnp.dot(x, wup[...], preferred_element_type=jnp.float32)
    hidden = (gpart * jax.nn.sigmoid(gpart) * upart).astype(jnp.bfloat16)
    return jnp.dot(hidden, wdown[...], preferred_element_type=jnp.float32).astype(jnp.bfloat16)


def slots_body(rows, gain, wgate, wup, wdown, after, *outs):
    part = expert(rows[...], gain, wgate, wup, wdown)
    width = outs[0].shape[1]
    for n, out in enumerate(outs):
        out[...] = part[:, n * width : (n + 1) * width]


def slots(rows, gain, weights, after, pieces):
    outs = [like((CAP, weights[2].shape[1] // pieces))] * pieces
    return call(slots_body, outs, (rows, gain, *weights, after), flops=6 * CAP * weights[0].size)


def tokens_body(k, rows, place, gain, wgate, wup, wdown, after, out):
    out[...] = expert(packed(place, k, rows), gain, wgate, wup, wdown)


def tokens(k, rows, place, gain, weights, after):
    outs = [like((CAP, weights[2].shape[1]))]
    ins = (rows, place, gain, *weights, after)
    return call(functools.partial(tokens_body, k), outs, ins, flops=6 * CAP * weights[0].size)[0]


STRIP = 256


def spread_body(which, count, first, *refs):
    bases, (place_t, weight_t, *parts), out = refs[:count], refs[count:-2], refs[-1]
    size, width = weight_t.shape[0], out.shape[1]
    for at in range(0, width, STRIP):
        strip = slice(at, at + STRIP)
        terms = [base[:, strip].astype(jnp.float32) for base in bases]
        for k, part in zip(which, parts):
            hit = place_t[k * size : (k + 1) * size, :]
            begin = at if part.shape[1] == width else first + at
            rows = jnp.dot(hit, part[:, begin : begin + STRIP], preferred_element_type=jnp.float32)
            terms.append(weight_t[:, k : k + 1] * rows)
        out[:, strip] = sum(terms[1:], terms[0]).astype(out.dtype)


def spread(which, bases, place_t, weight_t, parts, dtype, after, columns):
    outs = [like((weight_t.shape[0], columns.stop - columns.start), dtype)]
    body = functools.partial(spread_body, which, len(bases), columns.start)
    return call(body, outs, (*bases, place_t, weight_t, *parts, after))[0]


def added_body(total, left, right, out, here, done):
    half = left.shape[1]
    copies = []
    for n, at in enumerate(range(0, out.shape[1], WIDE)):
        strip = slice(at, at + WIDE)
        more = (left if at < half else right)[:, at % half : at % half + WIDE]
        here[:, strip] = (total[:, strip] + more.astype(jnp.float32)).astype(out.dtype)
        copies.append(pltpu.make_async_copy(here.at[:, pl.ds(at, WIDE)], out.at[:, pl.ds(at, WIDE)], done.at[n]))
        copies[-1].start()
    for copy in copies:
        copy.wait()


WIDE = 512


def added(total, left, right, dtype):
    out = like(total.shape, dtype)
    return pl.pallas_call(
        added_body,
        out_shape=out,
        in_specs=[spec()] * 3,
        out_specs=spec(pltpu.HBM),
        scratch_shapes=[VMEM(out.shape, dtype), pltpu.SemaphoreType.DMA((total.shape[1] // WIDE,))],
        compiler_params=pltpu.CompilerParams(vmem_limit_bytes=8 << 20),
        cost_estimate=pl.CostEstimate(flops=0, bytes_accessed=0, transcendentals=0),
    )(total, left, right)


def moved(value, back, flip):
    sections, experts = lax.axis_size("section"), lax.axis_size("expert")
    pairs = [
        ((s - back) % sections * experts + (e ^ flip(s)), s * experts + e)
        for s in range(sections)
        for e in range(experts)
    ]
    return lax.ppermute(value, ("section", "expert"), pairs)


def near_flip(section):
    return flips(section)[0]


def side_flip(section):
    return flips(section)[1]


LONG = 20_000_000_000


def local_square(acts, routes, gates, norm_gain, gate_w, up_w, down_w):
    weights = (gate_w[0], up_w[0], down_w[0])
    near_rows = moved(acts[0], 1, near_flip)
    table, gain = tabled(routes[0].T, gates[0].T, norm_gain)
    near_table = moved(table, 0, near_flip)
    place, place_t, weight_t, sent = routing(table, near_table, acts[0])
    rows = moved(sent, 1, lambda s: 0)
    onward = pack(NEAR_SIDE, near_rows, place, near_rows)
    far_rows = moved(onward, 0, side_flip)
    near_out = tokens(NEAR_HERE, near_rows, place, gain, weights, onward)
    side_send = pack(OWN_SIDE, rows, place, near_out)
    side_rows = moved(side_send, 0, side_flip)
    (far_out,) = slots(far_rows, gain, weights, side_send, 1)
    on_out = moved(far_out, 0, side_flip)
    (side_out,) = slots(side_rows, gain, weights, far_out, 1)
    from_side = moved(side_out, 0, side_flip)
    half, width = acts.shape[2] // 2, acts.shape[2]
    both = (NEAR_HERE, NEAR_SIDE)
    right = spread(both, (), place_t, weight_t, (near_out, on_out), jnp.bfloat16, side_out, slice(half, width))
    left = spread(both, (), place_t, weight_t, (near_out, on_out), jnp.bfloat16, right, slice(0, half))
    from_left = moved(left, 0, near_flip)
    from_right = moved(right, 0, near_flip)
    here = tokens(OWN_HERE, rows, place, gain, weights, left)
    parts = (here, from_side)
    total = spread((OWN_HERE, OWN_SIDE), (rows,), place_t, weight_t, parts, jnp.float32, here, slice(0, width))
    return added(total, from_left, from_right, acts.dtype)[None]


def solution(mesh):
    in_specs = (
        P("section", "expert", None),
        P("section", "expert", None),
        P("section", "expert", None),
        P("section", None),
        P("section", None, "expert"),
        P("section", None, "expert"),
        P("section", "expert", None),
    )
    out_specs = P("section", "expert", None)
    local = local_square if mesh.shape["expert"] == NEXP else local_any
    return jax.shard_map(local, mesh=mesh, in_specs=in_specs, out_specs=out_specs, check_vma=False)
```

```python
import functools

import jax
import jax.numpy as jnp
from jax import lax
from jax.experimental import pallas as pl
from jax.experimental.pallas import tpu as pltpu
from jax.sharding import PartitionSpec as P

NEXP = 4
CAP = 96
VMEM = pltpu.VMEM


def shifted(value, axis, steps):
    count = lax.axis_size(axis)
    pairs = [(source, (source + steps) % count) for source in range(count)]
    return lax.ppermute(value, axis, pairs)


def expert_rows(rows, wgate, wup, wdown):
    gpart = jnp.einsum("scd,dh->sch", rows, wgate, preferred_element_type=jnp.float32)
    upart = jnp.einsum("scd,dh->sch", rows, wup, preferred_element_type=jnp.float32)
    hidden = (jax.nn.silu(gpart) * upart).astype(jnp.bfloat16)
    return jnp.einsum("sch,hd->scd", hidden, wdown, preferred_element_type=jnp.float32).astype(
        jnp.bfloat16
    )


def local_any(acts, routes, gates, norm_gain, gate_w, up_w, down_w):
    arrived = shifted(acts, "section", 1)[0]
    ids = routes[0]
    weights = gates[0]
    gain = norm_gain[0]
    wgate = gate_w[0]
    wup = up_w[0]
    wdown = down_w[0]
    hsplit = lax.axis_size("expert") // NEXP
    tok_count = ids.shape[0]
    chosen = (ids[:, :, None] == jnp.arange(NEXP, dtype=jnp.int32)[None, None, :]).astype(jnp.int32)
    member = jnp.sum(chosen, axis=1)
    gate_of = jnp.sum(weights[:, :, None] * chosen.astype(jnp.float32), axis=1)
    slot_rank = jnp.cumsum(member, axis=0) - 1
    slots = jnp.arange(CAP, dtype=jnp.int32)
    place = (slot_rank.T[:, None, :] == slots[None, :, None]) & (member.T[:, None, :] > 0)
    place_bf = place.astype(jnp.bfloat16)
    xf = arrived.astype(jnp.float32)
    scale = lax.rsqrt(jnp.mean(xf * xf, axis=1, keepdims=True) + 1e-06)
    normed = (xf * scale * gain[None, :]).astype(jnp.bfloat16)
    packed = jnp.einsum("gct,td->gcd", place_bf, normed, preferred_element_type=jnp.float32).astype(
        jnp.bfloat16
    )
    outgoing = jnp.repeat(packed, hsplit, axis=0)
    received = lax.all_to_all(outgoing, "expert", split_axis=0, concat_axis=0, tiled=True)
    returned = lax.all_to_all(
        expert_rows(received, wgate, wup, wdown), "expert", split_axis=0, concat_axis=0, tiled=True
    )
    shards = returned.reshape(NEXP, hsplit, CAP, returned.shape[-1])
    per_expert = jnp.einsum("gct,ghcd->gtd", place_bf, shards, preferred_element_type=jnp.float32)
    contrib = jnp.sum(per_expert * gate_of.T[:, :, None], axis=0)
    result = (xf + contrib).astype(jnp.bfloat16)
    return result.reshape(1, tok_count, result.shape[-1])


def spec(space=VMEM):
    return pl.BlockSpec(memory_space=space)


def call(body, outs, ins, limit=16, flops=0, scratch=()):
    return pl.pallas_call(
        body,
        out_shape=outs,
        in_specs=[spec()] * len(ins),
        out_specs=[spec() for _ in outs],
        scratch_shapes=scratch,
        compiler_params=pltpu.CompilerParams(vmem_limit_bytes=limit << 20),
        cost_estimate=pl.CostEstimate(flops=flops, bytes_accessed=0, transcendentals=0),
    )(*ins)


def like(shape, dtype=jnp.bfloat16):
    return jax.ShapeDtypeStruct(shape, dtype)


def flips(section):
    odd = section % 2
    return 1 + odd, 2 - odd


def position():
    me = lax.axis_index("expert")
    return me, me ^ (2 - lax.rem(lax.axis_index("section"), 2))


def table_body(ids, gates, gain, table, gain_out, ids_here, gates_here, done):
    copies = [(ids, ids_here), (gates, gates_here), (gain, gain_out)]
    copies = [pltpu.make_async_copy(source, target, done.at[n]) for n, (source, target) in enumerate(copies)]
    for copy in copies:
        copy.start()
    for copy in copies:
        copy.wait()
    table[0:2, :] = ids_here[...].astype(jnp.float32)
    table[2:4, :] = gates_here[...]
    table[4:8, :] = jnp.zeros((4, table.shape[1]), jnp.float32)


def tabled(ids, gates, gain):
    ins = [pltpu.with_memory_space_constraint(v, pltpu.HBM) for v in (ids, gates, gain)]
    return pl.pallas_call(
        table_body,
        out_shape=[like((8, ids.shape[1]), jnp.float32), like(gain.shape, gain.dtype)],
        in_specs=[spec(pltpu.HBM)] * 3,
        out_specs=[spec()] * 2,
        scratch_shapes=[VMEM(ids.shape, ids.dtype), VMEM(gates.shape, gates.dtype), pltpu.SemaphoreType.DMA((3,))],
        compiler_params=pltpu.CompilerParams(vmem_limit_bytes=4 << 20),
        cost_estimate=pl.CostEstimate(flops=LONG, bytes_accessed=0, transcendentals=0),
    )(*ins)


PACKED = OWN_HERE, OWN_SIDE, NEAR_HERE, NEAR_SIDE = range(4)
BACK_HERE, BACK_LEFT, BACK_RIGHT, LEFT_HERE, LEFT_ON, RIGHT_HERE, RIGHT_ON = range(7)


def routing_body(own, near, beside, place, place_t, weight_t):
    me, side = position()
    odd = lax.rem(lax.axis_index("section"), 2)
    other = side ^ (3 - 3 * odd)
    third = jnp.where(odd == 1, near[...], beside[...])
    own, near = own[...], near[...]
    ask = [(own, me), (own, side), (own, other), (near, me), (near, side), (third, me), (third, other)]
    names = [(table[0:1, :] == g.astype(jnp.float32), table[1:2, :] == g.astype(jnp.float32)) for table, g in ask]
    rows = [(first | second).astype(jnp.float32) for first, second in names]
    member = jnp.concatenate(rows + [jnp.zeros_like(rows[0])] * (8 - len(rows)), axis=0)
    tokens = member.shape[1]
    before = lax.broadcasted_iota(jnp.int32, (tokens, tokens), 0)
    at = lax.broadcasted_iota(jnp.int32, (tokens, tokens), 1)
    upto = (before <= at).astype(jnp.bfloat16)
    rank = jnp.dot(member.astype(jnp.bfloat16), upto, preferred_element_type=jnp.float32) - 1.0
    slots = lax.broadcasted_iota(jnp.int32, (CAP, tokens), 0).astype(jnp.float32)
    lanes = lax.broadcasted_iota(jnp.int32, (tokens, CAP), 1).astype(jnp.float32)
    member_t, rank_t = member.T, rank.T
    for n, k in enumerate((BACK_HERE, BACK_LEFT, LEFT_HERE, LEFT_ON)):
        hit = (slots == rank[k : k + 1, :]) & (member[k : k + 1, :] > 0)
        place[n * CAP : (n + 1) * CAP, :] = hit.astype(jnp.bfloat16)
    for k in range(len(ask)):
        hit = (lanes == rank_t[:, k : k + 1]) & (member_t[:, k : k + 1] > 0)
        place_t[k * tokens : (k + 1) * tokens, :] = hit.astype(jnp.bfloat16)
    weight = [
        jnp.where(first, table[2:3, :], 0.0) + jnp.where(second, table[3:4, :], 0.0)
        for (table, _), (first, second) in zip(ask, names)
    ]
    weight_t[...] = jnp.concatenate(weight + [jnp.zeros_like(weight[0])] * (8 - len(weight)), axis=0).T


def routing(own, near, side):
    tokens = own.shape[1]
    outs = [like((len(PACKED) * CAP, tokens)), like((7 * tokens, CAP)), like((tokens, 8), jnp.float32)]
    return call(routing_body, outs, (own, near, side))


def packed(place, k, rows):
    hit = place[k * CAP : (k + 1) * CAP, :]
    return jnp.dot(hit, rows[...], preferred_element_type=jnp.float32).astype(jnp.bfloat16)


def pack_body(k, rows, place, after, out):
    out[...] = packed(place, k, rows)


def pack(k, rows, place, after):
    return call(functools.partial(pack_body, k), [like((CAP, rows.shape[1]))], (rows, place, after))[0]


def expert(rows, gain, wgate, wup, wdown):
    xf = rows.astype(jnp.float32)
    scale = lax.rsqrt(jnp.mean(xf * xf, axis=1, keepdims=True) + 1e-06)
    x = (xf * scale * gain[...]).astype(jnp.bfloat16)
    gpart = jnp.dot(x, wgate[...], preferred_element_type=jnp.float32)
    upart = jnp.dot(x, wup[...], preferred_element_type=jnp.float32)
    hidden = (gpart * jax.nn.sigmoid(gpart) * upart).astype(jnp.bfloat16)
    return jnp.dot(hidden, wdown[...], preferred_element_type=jnp.float32).astype(jnp.bfloat16)


def slots_body(rows, gain, wgate, wup, wdown, after, left, right):
    part = expert(rows[...], gain, wgate, wup, wdown)
    left[...] = part[:, : left.shape[1]]
    right[...] = part[:, left.shape[1] :]


def slots(rows, gain, weights, after, cut):
    outs = [like((CAP, cut)), like((CAP, weights[2].shape[1] - cut))]
    return call(slots_body, outs, (rows, gain, *weights, after), flops=6 * CAP * weights[0].size)


def side_body(rows, gain, wgate, wup, wdown, near_out, after, left, right, keep):
    part = expert(rows[...], gain, wgate, wup, wdown)
    half = left.shape[1]
    odd = lax.rem(lax.axis_index("section"), 2) == 1
    left[...] = part[:, :half]
    right[...] = jnp.where(odd, part[:, half:], near_out[:, half:])
    keep[...] = jnp.where(odd, near_out[:, half:], part[:, half:])


def sided(rows, gain, weights, near_out, after, cut):
    rest = like((CAP, weights[2].shape[1] - cut))
    outs = [like((CAP, cut)), rest, rest]
    return call(side_body, outs, (rows, gain, *weights, near_out, after), flops=6 * CAP * weights[0].size)


def tokens_body(k, rows, place, gain, wgate, wup, wdown, after, out):
    out[...] = expert(packed(place, k, rows), gain, wgate, wup, wdown)


def tokens(k, rows, place, gain, weights, after):
    outs = [like((CAP, weights[2].shape[1]))]
    ins = (rows, place, gain, *weights, after)
    return call(functools.partial(tokens_body, k), outs, ins, flops=6 * CAP * weights[0].size)[0]


STRIP = 256


def spread_body(which, count, first, *refs):
    bases, (place_t, weight_t, *parts), out = refs[:count], refs[count:-2], refs[-1]
    size, width = weight_t.shape[0], out.shape[1]
    for at in range(0, width, STRIP):
        strip = slice(at, at + STRIP)
        terms = [base[:, strip].astype(jnp.float32) for base in bases]
        for k, part in zip(which, parts):
            hit = place_t[k * size : (k + 1) * size, :]
            begin = at if part.shape[1] == width else first + at
            rows = jnp.dot(hit, part[:, begin : begin + STRIP], preferred_element_type=jnp.float32)
            terms.append(weight_t[:, k : k + 1] * rows)
        out[:, strip] = sum(terms[1:], terms[0]).astype(out.dtype)


def spread(which, bases, place_t, weight_t, parts, dtype, after, columns, flops=0):
    outs = [like((weight_t.shape[0], columns.stop - columns.start), dtype)]
    body = functools.partial(spread_body, which, len(bases), columns.start)
    return call(body, outs, (*bases, place_t, weight_t, *parts, after), flops=flops)[0]


def based_body(rows, place_t, weight_t, here, left, out):
    half, size = left.shape[1], weight_t.shape[0]
    for at in range(0, out.shape[1], STRIP):
        strip = slice(at, at + STRIP)
        total = rows[:, strip].astype(jnp.float32)
        for k, part in ((BACK_HERE, here), (BACK_LEFT, left)):
            if at < half or k == BACK_HERE:
                hit = place_t[k * size : (k + 1) * size, :]
                slots_here = jnp.dot(hit, part[:, strip], preferred_element_type=jnp.float32)
                total = total + weight_t[:, k : k + 1] * slots_here
        out[:, strip] = total


def based(rows, place_t, weight_t, here, left):
    return call(based_body, [like(rows.shape, jnp.float32)], (rows, place_t, weight_t, here, left), flops=LONG)[0]


def last_body(base, place_t, weight_t, slots_right, left, right, out, here, done):
    half, size = left.shape[1], weight_t.shape[0]
    hit = place_t[BACK_RIGHT * size : (BACK_RIGHT + 1) * size, :]
    weight = weight_t[:, BACK_RIGHT : BACK_RIGHT + 1]
    copies = []
    for n, at in enumerate(range(0, out.shape[1], WIDE)):
        for begin in range(at, at + WIDE, STRIP):
            first = begin if begin < half else begin - half
            strip, within = slice(begin, begin + STRIP), slice(first, first + STRIP)
            total = base[:, strip] + (left if begin < half else right)[:, within].astype(jnp.float32)
            if begin >= half:
                total += weight * jnp.dot(hit, slots_right[:, within], preferred_element_type=jnp.float32)
            here[:, strip] = total.astype(out.dtype)
        copies.append(pltpu.make_async_copy(here.at[:, pl.ds(at, WIDE)], out.at[:, pl.ds(at, WIDE)], done.at[n]))
        copies[-1].start()
    for copy in copies:
        copy.wait()


WIDE = 256


def last(base, place_t, weight_t, slots_right, left, right, dtype):
    out = like(base.shape, dtype)
    return pl.pallas_call(
        last_body,
        out_shape=out,
        in_specs=[spec()] * 6,
        out_specs=spec(pltpu.HBM),
        scratch_shapes=[VMEM(out.shape, dtype), pltpu.SemaphoreType.DMA((base.shape[1] // WIDE,))],
        compiler_params=pltpu.CompilerParams(vmem_limit_bytes=8 << 20),
        cost_estimate=pl.CostEstimate(flops=0, bytes_accessed=0, transcendentals=0),
    )(base, place_t, weight_t, slots_right, left, right)


def moved(value, back, flip):
    sections, experts = lax.axis_size("section"), lax.axis_size("expert")
    pairs = [
        ((s - back) % sections * experts + (e ^ flip(s)), s * experts + e)
        for s in range(sections)
        for e in range(experts)
    ]
    return lax.ppermute(value, ("section", "expert"), pairs)


def near_flip(section):
    return flips(section)[0]


def side_flip(section):
    return flips(section)[1]


LONG = 20_000_000_000
CUT = 5


def local_square(acts, routes, gates, norm_gain, gate_w, up_w, down_w):
    weights = (gate_w[0], up_w[0], down_w[0])
    near_rows = moved(acts[0], 1, near_flip)
    rows = moved(acts[0], 1, lambda s: 0)
    table, gain = tabled(routes[0].T, gates[0].T, norm_gain)
    near_table = moved(table, 0, near_flip)
    side_table = moved(table, 0, side_flip)
    place, place_t, weight_t = routing(table, near_table, side_table)
    onward = pack(NEAR_SIDE, near_rows, place, near_rows)
    far_rows = moved(onward, 0, side_flip)
    near_out = tokens(NEAR_HERE, near_rows, place, gain, weights, onward)
    side_send = pack(OWN_SIDE, rows, place, near_out)
    side_rows = moved(side_send, 0, side_flip)
    width = acts.shape[2]
    cut = width * CUT // 8
    far_left, far_right = slots(far_rows, gain, weights, side_send, cut)
    on_left = moved(far_left, 0, side_flip)
    on_right = moved(far_right, 0, lambda s: side_flip(s) if s % 2 else near_flip(s))
    left_slots, right_slots, keep = sided(side_rows, gain, weights, near_out, far_left, cut)
    left_slots = moved(left_slots, 0, side_flip)
    right_slots = moved(right_slots, 0, lambda s: side_flip(s) if s % 2 else near_flip(s))
    left = spread((LEFT_HERE, LEFT_ON), (), place_t, weight_t, (near_out, on_left), jnp.bfloat16, keep, slice(0, cut))
    right = spread((RIGHT_HERE, RIGHT_ON), (), place_t, weight_t, (keep, on_right), jnp.bfloat16, left, slice(cut, width))
    from_left = moved(left, 0, near_flip)
    from_right = moved(right, 0, lambda s: near_flip(s) if s % 2 else side_flip(s))
    here = tokens(OWN_HERE, rows, place, gain, weights, right)
    base = based(rows, place_t, weight_t, here, left_slots)
    return last(base, place_t, weight_t, right_slots, from_left, from_right, acts.dtype)[None]


def solution(mesh):
    in_specs = (
        P("section", "expert", None),
        P("section", "expert", None),
        P("section", "expert", None),
        P("section", None),
        P("section", None, "expert"),
        P("section", None, "expert"),
        P("section", "expert", None),
    )
    out_specs = P("section", "expert", None)
    local = local_square if mesh.shape["expert"] == NEXP else local_any
    return jax.shard_map(local, mesh=mesh, in_specs=in_specs, out_specs=out_specs, check_vma=False)
```

```python
import functools

import jax
import jax.numpy as jnp
from jax import lax
from jax.experimental import pallas as pl
from jax.experimental.pallas import tpu as pltpu
from jax.sharding import PartitionSpec as P

NEXP = 4
CAP = 96
VMEM = pltpu.VMEM


def shifted(value, axis, steps):
    count = lax.axis_size(axis)
    pairs = [(source, (source + steps) % count) for source in range(count)]
    return lax.ppermute(value, axis, pairs)


def expert_rows(rows, wgate, wup, wdown):
    gpart = jnp.einsum("scd,dh->sch", rows, wgate, preferred_element_type=jnp.float32)
    upart = jnp.einsum("scd,dh->sch", rows, wup, preferred_element_type=jnp.float32)
    hidden = (jax.nn.silu(gpart) * upart).astype(jnp.bfloat16)
    return jnp.einsum("sch,hd->scd", hidden, wdown, preferred_element_type=jnp.float32).astype(
        jnp.bfloat16
    )


def local_any(acts, routes, gates, norm_gain, gate_w, up_w, down_w):
    arrived = shifted(acts, "section", 1)[0]
    ids = routes[0]
    weights = gates[0]
    gain = norm_gain[0]
    wgate = gate_w[0]
    wup = up_w[0]
    wdown = down_w[0]
    hsplit = lax.axis_size("expert") // NEXP
    tok_count = ids.shape[0]
    chosen = (ids[:, :, None] == jnp.arange(NEXP, dtype=jnp.int32)[None, None, :]).astype(jnp.int32)
    member = jnp.sum(chosen, axis=1)
    gate_of = jnp.sum(weights[:, :, None] * chosen.astype(jnp.float32), axis=1)
    slot_rank = jnp.cumsum(member, axis=0) - 1
    slots = jnp.arange(CAP, dtype=jnp.int32)
    place = (slot_rank.T[:, None, :] == slots[None, :, None]) & (member.T[:, None, :] > 0)
    place_bf = place.astype(jnp.bfloat16)
    xf = arrived.astype(jnp.float32)
    scale = lax.rsqrt(jnp.mean(xf * xf, axis=1, keepdims=True) + 1e-06)
    normed = (xf * scale * gain[None, :]).astype(jnp.bfloat16)
    packed = jnp.einsum("gct,td->gcd", place_bf, normed, preferred_element_type=jnp.float32).astype(
        jnp.bfloat16
    )
    outgoing = jnp.repeat(packed, hsplit, axis=0)
    received = lax.all_to_all(outgoing, "expert", split_axis=0, concat_axis=0, tiled=True)
    returned = lax.all_to_all(
        expert_rows(received, wgate, wup, wdown), "expert", split_axis=0, concat_axis=0, tiled=True
    )
    shards = returned.reshape(NEXP, hsplit, CAP, returned.shape[-1])
    per_expert = jnp.einsum("gct,ghcd->gtd", place_bf, shards, preferred_element_type=jnp.float32)
    contrib = jnp.sum(per_expert * gate_of.T[:, :, None], axis=0)
    result = (xf + contrib).astype(jnp.bfloat16)
    return result.reshape(1, tok_count, result.shape[-1])


def spec(space=VMEM):
    return pl.BlockSpec(memory_space=space)


def call(body, outs, ins, limit=16, flops=0, scratch=()):
    return pl.pallas_call(
        body,
        out_shape=outs,
        in_specs=[spec()] * len(ins),
        out_specs=[spec() for _ in outs],
        scratch_shapes=scratch,
        compiler_params=pltpu.CompilerParams(vmem_limit_bytes=limit << 20),
        cost_estimate=pl.CostEstimate(flops=flops, bytes_accessed=0, transcendentals=0),
    )(*ins)


def like(shape, dtype=jnp.bfloat16):
    return jax.ShapeDtypeStruct(shape, dtype)


def flips(section):
    odd = section % 2
    return 1 + odd, 2 - odd


def position():
    me = lax.axis_index("expert")
    return me, me ^ (2 - lax.rem(lax.axis_index("section"), 2))


def table_body(ids, gates, gain, table, gain_out, ids_here, gates_here, done):
    copies = [(ids, ids_here), (gates, gates_here), (gain, gain_out)]
    copies = [pltpu.make_async_copy(source, target, done.at[n]) for n, (source, target) in enumerate(copies)]
    for copy in copies:
        copy.start()
    for copy in copies:
        copy.wait()
    table[0:2, :] = ids_here[...].astype(jnp.float32)
    table[2:4, :] = gates_here[...]
    table[4:8, :] = jnp.zeros((4, table.shape[1]), jnp.float32)


def tabled(ids, gates, gain):
    ins = [pltpu.with_memory_space_constraint(v, pltpu.HBM) for v in (ids, gates, gain)]
    return pl.pallas_call(
        table_body,
        out_shape=[like((8, ids.shape[1]), jnp.float32), like(gain.shape, gain.dtype)],
        in_specs=[spec(pltpu.HBM)] * 3,
        out_specs=[spec()] * 2,
        scratch_shapes=[VMEM(ids.shape, ids.dtype), VMEM(gates.shape, gates.dtype), pltpu.SemaphoreType.DMA((3,))],
        compiler_params=pltpu.CompilerParams(vmem_limit_bytes=4 << 20),
        cost_estimate=pl.CostEstimate(flops=LONG, bytes_accessed=0, transcendentals=0),
    )(*ins)


PACKED = OWN_HERE, OWN_SIDE, NEAR_HERE, NEAR_SIDE = range(4)
BACK_HERE, BACK_LEFT, BACK_RIGHT, LEFT_HERE, LEFT_ON, RIGHT_HERE, RIGHT_ON = range(7)


def routing_body(own, near, beside, place, place_t, weight_t):
    me, side = position()
    odd = lax.rem(lax.axis_index("section"), 2)
    other = side ^ (3 - 3 * odd)
    third = jnp.where(odd == 1, near[...], beside[...])
    own, near = own[...], near[...]
    ask = [(own, me), (own, side), (own, other), (near, me), (near, side), (third, me), (third, other)]
    names = [(table[0:1, :] == g.astype(jnp.float32), table[1:2, :] == g.astype(jnp.float32)) for table, g in ask]
    rows = [(first | second).astype(jnp.float32) for first, second in names]
    member = jnp.concatenate(rows + [jnp.zeros_like(rows[0])] * (8 - len(rows)), axis=0)
    tokens = member.shape[1]
    before = lax.broadcasted_iota(jnp.int32, (tokens, tokens), 0)
    at = lax.broadcasted_iota(jnp.int32, (tokens, tokens), 1)
    upto = (before <= at).astype(jnp.bfloat16)
    rank = jnp.dot(member.astype(jnp.bfloat16), upto, preferred_element_type=jnp.float32) - 1.0
    slots = lax.broadcasted_iota(jnp.int32, (CAP, tokens), 0).astype(jnp.float32)
    lanes = lax.broadcasted_iota(jnp.int32, (tokens, CAP), 1).astype(jnp.float32)
    member_t, rank_t = member.T, rank.T
    for n, k in enumerate((BACK_HERE, BACK_LEFT, LEFT_HERE, LEFT_ON)):
        hit = (slots == rank[k : k + 1, :]) & (member[k : k + 1, :] > 0)
        place[n * CAP : (n + 1) * CAP, :] = hit.astype(jnp.bfloat16)
    for k in range(len(ask)):
        hit = (lanes == rank_t[:, k : k + 1]) & (member_t[:, k : k + 1] > 0)
        place_t[k * tokens : (k + 1) * tokens, :] = hit.astype(jnp.bfloat16)
    weight = [
        jnp.where(first, table[2:3, :], 0.0) + jnp.where(second, table[3:4, :], 0.0)
        for (table, _), (first, second) in zip(ask, names)
    ]
    weight_t[...] = jnp.concatenate(weight + [jnp.zeros_like(weight[0])] * (8 - len(weight)), axis=0).T


def routing(own, near, side):
    tokens = own.shape[1]
    outs = [like((len(PACKED) * CAP, tokens)), like((7 * tokens, CAP)), like((tokens, 8), jnp.float32)]
    return call(routing_body, outs, (own, near, side))


def packed(place, k, rows):
    hit = place[k * CAP : (k + 1) * CAP, :]
    return jnp.dot(hit, rows[...], preferred_element_type=jnp.float32).astype(jnp.bfloat16)


def pack_body(k, rows, place, after, out):
    out[...] = packed(place, k, rows)


def pack(k, rows, place, after):
    return call(functools.partial(pack_body, k), [like((CAP, rows.shape[1]))], (rows, place, after))[0]


def expert(rows, gain, wgate, wup, wdown):
    xf = rows.astype(jnp.float32)
    scale = lax.rsqrt(jnp.mean(xf * xf, axis=1, keepdims=True) + 1e-06)
    x = (xf * scale * gain[...]).astype(jnp.bfloat16)
    gpart = jnp.dot(x, wgate[...], preferred_element_type=jnp.float32)
    upart = jnp.dot(x, wup[...], preferred_element_type=jnp.float32)
    hidden = (gpart * jax.nn.sigmoid(gpart) * upart).astype(jnp.bfloat16)
    return jnp.dot(hidden, wdown[...], preferred_element_type=jnp.float32).astype(jnp.bfloat16)


def slots_body(rows, gain, wgate, wup, wdown, after, left, right):
    part = expert(rows[...], gain, wgate, wup, wdown)
    left[...] = part[:, : left.shape[1]]
    right[...] = part[:, left.shape[1] :]


def slots(rows, gain, weights, after, cut):
    outs = [like((CAP, cut)), like((CAP, weights[2].shape[1] - cut))]
    return call(slots_body, outs, (rows, gain, *weights, after), flops=6 * CAP * weights[0].size)


def side_body(rows, gain, wgate, wup, wdown, near_out, after, left, right, keep):
    part = expert(rows[...], gain, wgate, wup, wdown)
    half = left.shape[1]
    odd = lax.rem(lax.axis_index("section"), 2) == 1
    left[...] = part[:, :half]
    right[...] = jnp.where(odd, part[:, half:], near_out[:, half:])
    keep[...] = jnp.where(odd, near_out[:, half:], part[:, half:])


def sided(rows, gain, weights, near_out, after, cut):
    rest = like((CAP, weights[2].shape[1] - cut))
    outs = [like((CAP, cut)), rest, rest]
    return call(side_body, outs, (rows, gain, *weights, near_out, after), flops=6 * CAP * weights[0].size)


def tokens_body(k, rows, place, gain, wgate, wup, wdown, after, out):
    out[...] = expert(packed(place, k, rows), gain, wgate, wup, wdown)


def tokens(k, rows, place, gain, weights, after):
    outs = [like((CAP, weights[2].shape[1]))]
    ins = (rows, place, gain, *weights, after)
    return call(functools.partial(tokens_body, k), outs, ins, flops=6 * CAP * weights[0].size)[0]


STRIP = 256


def spread_body(which, count, first, *refs):
    bases, (place_t, weight_t, *parts), out = refs[:count], refs[count:-2], refs[-1]
    size, width = weight_t.shape[0], out.shape[1]
    for at in range(0, width, STRIP):
        strip = slice(at, at + STRIP)
        terms = [base[:, strip].astype(jnp.float32) for base in bases]
        for k, part in zip(which, parts):
            hit = place_t[k * size : (k + 1) * size, :]
            begin = at if part.shape[1] == width else first + at
            rows = jnp.dot(hit, part[:, begin : begin + STRIP], preferred_element_type=jnp.float32)
            terms.append(weight_t[:, k : k + 1] * rows)
        out[:, strip] = sum(terms[1:], terms[0]).astype(out.dtype)


def spread(which, bases, place_t, weight_t, parts, dtype, after, columns, flops=0):
    outs = [like((weight_t.shape[0], columns.stop - columns.start), dtype)]
    body = functools.partial(spread_body, which, len(bases), columns.start)
    return call(body, outs, (*bases, place_t, weight_t, *parts, after), flops=flops)[0]


def based_body(rows, place_t, weight_t, here, left, out):
    half, size = left.shape[1], weight_t.shape[0]
    for at in range(0, out.shape[1], STRIP):
        strip = slice(at, at + STRIP)
        total = rows[:, strip].astype(jnp.float32)
        for k, part in ((BACK_HERE, here), (BACK_LEFT, left)):
            if at < half or k == BACK_HERE:
                hit = place_t[k * size : (k + 1) * size, :]
                slots_here = jnp.dot(hit, part[:, strip], preferred_element_type=jnp.float32)
                total = total + weight_t[:, k : k + 1] * slots_here
        out[:, strip] = total


def based(rows, place_t, weight_t, here, left):
    return call(based_body, [like(rows.shape, jnp.float32)], (rows, place_t, weight_t, here, left), flops=LONG)[0]


def written(value, here, out, first, done, n):
    width = value.shape[1]
    here[:, first : first + width] = value.astype(out.dtype)
    copy = pltpu.make_async_copy(here.at[:, pl.ds(first, width)], out.at[:, pl.ds(first, width)], done.at[n])
    copy.start()
    return copy


def first_body(base, place_t, weight_t, slots_right, left, out, rest, here, done):
    cut, size = left.shape[1], weight_t.shape[0]
    copies = []
    for n, at in enumerate(range(0, cut, STRIP)):
        strip = slice(at, at + STRIP)
        copies.append(written(base[:, strip] + left[:, strip].astype(jnp.float32), here, out, at, done, n))
    hit = place_t[BACK_RIGHT * size : (BACK_RIGHT + 1) * size, :]
    weight = weight_t[:, BACK_RIGHT : BACK_RIGHT + 1]
    for at in range(0, rest.shape[1], STRIP):
        strip = slice(at, at + STRIP)
        rows = jnp.dot(hit, slots_right[:, strip], preferred_element_type=jnp.float32)
        rest[:, strip] = base[:, cut + at : cut + at + STRIP] + weight * rows
    for copy in copies:
        copy.wait()


def rest_body(_, rest, right, out, here, done):
    cut = out.shape[1] - rest.shape[1]
    copies = []
    for n, at in enumerate(range(0, rest.shape[1], STRIP)):
        strip = slice(at, at + STRIP)
        copies.append(written(rest[:, strip] + right[:, strip].astype(jnp.float32), here, out, cut + at, done, n))
    for copy in copies:
        copy.wait()


def last(base, place_t, weight_t, slots_right, left, right, dtype):
    out = like(base.shape, dtype)
    rest = like(right.shape, jnp.float32)
    common = dict(
        scratch_shapes=[VMEM(out.shape, dtype), pltpu.SemaphoreType.DMA((base.shape[1] // STRIP,))],
        compiler_params=pltpu.CompilerParams(vmem_limit_bytes=8 << 20),
        cost_estimate=pl.CostEstimate(flops=0, bytes_accessed=0, transcendentals=0),
    )
    result, rest = pl.pallas_call(
        first_body,
        out_shape=[out, rest],
        in_specs=[spec()] * 5,
        out_specs=[spec(pltpu.HBM), spec()],
        **common,
    )(base, place_t, weight_t, slots_right, left)
    return pl.pallas_call(
        rest_body,
        out_shape=out,
        in_specs=[spec(pltpu.HBM)] + [spec()] * 2,
        out_specs=spec(pltpu.HBM),
        input_output_aliases={0: 0},
        **common,
    )(result, rest, right)


def moved(value, back, flip):
    sections, experts = lax.axis_size("section"), lax.axis_size("expert")
    pairs = [
        ((s - back) % sections * experts + (e ^ flip(s)), s * experts + e)
        for s in range(sections)
        for e in range(experts)
    ]
    return lax.ppermute(value, ("section", "expert"), pairs)


def near_flip(section):
    return flips(section)[0]


def side_flip(section):
    return flips(section)[1]


LONG = 20_000_000_000
CUT = 5


def local_square(acts, routes, gates, norm_gain, gate_w, up_w, down_w):
    weights = (gate_w[0], up_w[0], down_w[0])
    near_rows = moved(acts[0], 1, near_flip)
    rows = moved(acts[0], 1, lambda s: 0)
    table, gain = tabled(routes[0].T, gates[0].T, norm_gain)
    near_table = moved(table, 0, near_flip)
    side_table = moved(table, 0, side_flip)
    place, place_t, weight_t = routing(table, near_table, side_table)
    onward = pack(NEAR_SIDE, near_rows, place, near_rows)
    far_rows = moved(onward, 0, side_flip)
    near_out = tokens(NEAR_HERE, near_rows, place, gain, weights, onward)
    side_send = pack(OWN_SIDE, rows, place, near_out)
    side_rows = moved(side_send, 0, side_flip)
    width = acts.shape[2]
    cut = width * CUT // 8
    far_left, far_right = slots(far_rows, gain, weights, side_send, cut)
    on_left = moved(far_left, 0, side_flip)
    on_right = moved(far_right, 0, lambda s: side_flip(s) if s % 2 else near_flip(s))
    left_slots, right_slots, keep = sided(side_rows, gain, weights, near_out, far_left, cut)
    left_slots = moved(left_slots, 0, side_flip)
    right_slots = moved(right_slots, 0, lambda s: side_flip(s) if s % 2 else near_flip(s))
    left = spread((LEFT_HERE, LEFT_ON), (), place_t, weight_t, (near_out, on_left), jnp.bfloat16, keep, slice(0, cut))
    right = spread((RIGHT_HERE, RIGHT_ON), (), place_t, weight_t, (keep, on_right), jnp.bfloat16, left, slice(cut, width))
    from_left = moved(left, 0, near_flip)
    from_right = moved(right, 0, lambda s: near_flip(s) if s % 2 else side_flip(s))
    here = tokens(OWN_HERE, rows, place, gain, weights, right)
    base = based(rows, place_t, weight_t, here, left_slots)
    return last(base, place_t, weight_t, right_slots, from_left, from_right, acts.dtype)[None]


def solution(mesh):
    in_specs = (
        P("section", "expert", None),
        P("section", "expert", None),
        P("section", "expert", None),
        P("section", None),
        P("section", None, "expert"),
        P("section", None, "expert"),
        P("section", "expert", None),
    )
    out_specs = P("section", "expert", None)
    local = local_square if mesh.shape["expert"] == NEXP else local_any
    return jax.shard_map(local, mesh=mesh, in_specs=in_specs, out_specs=out_specs, check_vma=False)
```

```python
import functools

import jax
import jax.numpy as jnp
from jax import lax
from jax.experimental import pallas as pl
from jax.experimental.pallas import tpu as pltpu
from jax.sharding import PartitionSpec as P

NEXP = 4
CAP = 96
VMEM = pltpu.VMEM


def shifted(value, axis, steps):
    count = lax.axis_size(axis)
    pairs = [(source, (source + steps) % count) for source in range(count)]
    return lax.ppermute(value, axis, pairs)


def expert_rows(rows, wgate, wup, wdown):
    gpart = jnp.einsum("scd,dh->sch", rows, wgate, preferred_element_type=jnp.float32)
    upart = jnp.einsum("scd,dh->sch", rows, wup, preferred_element_type=jnp.float32)
    hidden = (jax.nn.silu(gpart) * upart).astype(jnp.bfloat16)
    return jnp.einsum("sch,hd->scd", hidden, wdown, preferred_element_type=jnp.float32).astype(
        jnp.bfloat16
    )


def local_any(acts, routes, gates, norm_gain, gate_w, up_w, down_w):
    arrived = shifted(acts, "section", 1)[0]
    ids = routes[0]
    weights = gates[0]
    gain = norm_gain[0]
    wgate = gate_w[0]
    wup = up_w[0]
    wdown = down_w[0]
    hsplit = lax.axis_size("expert") // NEXP
    tok_count = ids.shape[0]
    chosen = (ids[:, :, None] == jnp.arange(NEXP, dtype=jnp.int32)[None, None, :]).astype(jnp.int32)
    member = jnp.sum(chosen, axis=1)
    gate_of = jnp.sum(weights[:, :, None] * chosen.astype(jnp.float32), axis=1)
    slot_rank = jnp.cumsum(member, axis=0) - 1
    slots = jnp.arange(CAP, dtype=jnp.int32)
    place = (slot_rank.T[:, None, :] == slots[None, :, None]) & (member.T[:, None, :] > 0)
    place_bf = place.astype(jnp.bfloat16)
    xf = arrived.astype(jnp.float32)
    scale = lax.rsqrt(jnp.mean(xf * xf, axis=1, keepdims=True) + 1e-06)
    normed = (xf * scale * gain[None, :]).astype(jnp.bfloat16)
    packed = jnp.einsum("gct,td->gcd", place_bf, normed, preferred_element_type=jnp.float32).astype(
        jnp.bfloat16
    )
    outgoing = jnp.repeat(packed, hsplit, axis=0)
    received = lax.all_to_all(outgoing, "expert", split_axis=0, concat_axis=0, tiled=True)
    returned = lax.all_to_all(
        expert_rows(received, wgate, wup, wdown), "expert", split_axis=0, concat_axis=0, tiled=True
    )
    shards = returned.reshape(NEXP, hsplit, CAP, returned.shape[-1])
    per_expert = jnp.einsum("gct,ghcd->gtd", place_bf, shards, preferred_element_type=jnp.float32)
    contrib = jnp.sum(per_expert * gate_of.T[:, :, None], axis=0)
    result = (xf + contrib).astype(jnp.bfloat16)
    return result.reshape(1, tok_count, result.shape[-1])


def spec(space=VMEM):
    return pl.BlockSpec(memory_space=space)


def call(body, outs, ins, limit=16, flops=0, scratch=()):
    return pl.pallas_call(
        body,
        out_shape=outs,
        in_specs=[spec()] * len(ins),
        out_specs=[spec() for _ in outs],
        scratch_shapes=scratch,
        compiler_params=pltpu.CompilerParams(vmem_limit_bytes=limit << 20),
        cost_estimate=pl.CostEstimate(flops=flops, bytes_accessed=0, transcendentals=0),
    )(*ins)


def like(shape, dtype=jnp.bfloat16):
    return jax.ShapeDtypeStruct(shape, dtype)


def flips(section):
    odd = section % 2
    return 1 + odd, 2 - odd


def position():
    me = lax.axis_index("expert")
    return me, me ^ (2 - lax.rem(lax.axis_index("section"), 2))


def table_body(ids, gates, gain, table, gain_out, ids_here, gates_here, done):
    copies = [(ids, ids_here), (gates, gates_here), (gain, gain_out)]
    copies = [pltpu.make_async_copy(source, target, done.at[n]) for n, (source, target) in enumerate(copies)]
    for copy in copies:
        copy.start()
    for copy in copies:
        copy.wait()
    table[0:2, :] = ids_here[...].astype(jnp.float32)
    table[2:4, :] = gates_here[...]
    table[4:8, :] = jnp.zeros((4, table.shape[1]), jnp.float32)


def tabled(ids, gates, gain):
    ins = [pltpu.with_memory_space_constraint(v, pltpu.HBM) for v in (ids, gates, gain)]
    return pl.pallas_call(
        table_body,
        out_shape=[like((8, ids.shape[1]), jnp.float32), like(gain.shape, gain.dtype)],
        in_specs=[spec(pltpu.HBM)] * 3,
        out_specs=[spec()] * 2,
        scratch_shapes=[VMEM(ids.shape, ids.dtype), VMEM(gates.shape, gates.dtype), pltpu.SemaphoreType.DMA((3,))],
        compiler_params=pltpu.CompilerParams(vmem_limit_bytes=4 << 20),
        cost_estimate=pl.CostEstimate(flops=LONG, bytes_accessed=0, transcendentals=0),
    )(*ins)


PACKED = OWN_HERE, OWN_SIDE, NEAR_HERE, NEAR_SIDE = range(4)
BACK_HERE, BACK_LEFT, BACK_RIGHT, LEFT_HERE, LEFT_ON, RIGHT_HERE, RIGHT_ON = range(7)


def routing_body(own, near, beside, place, place_t, weight_t):
    me, side = position()
    odd = lax.rem(lax.axis_index("section"), 2)
    other = side ^ (3 - 3 * odd)
    third = jnp.where(odd == 1, near[...], beside[...])
    own, near = own[...], near[...]
    ask = [(own, me), (own, side), (own, other), (near, me), (near, side), (third, me), (third, other)]
    names = [(table[0:1, :] == g.astype(jnp.float32), table[1:2, :] == g.astype(jnp.float32)) for table, g in ask]
    rows = [(first | second).astype(jnp.float32) for first, second in names]
    member = jnp.concatenate(rows + [jnp.zeros_like(rows[0])] * (8 - len(rows)), axis=0)
    tokens = member.shape[1]
    before = lax.broadcasted_iota(jnp.int32, (tokens, tokens), 0)
    at = lax.broadcasted_iota(jnp.int32, (tokens, tokens), 1)
    upto = (before <= at).astype(jnp.bfloat16)
    rank = jnp.dot(member.astype(jnp.bfloat16), upto, preferred_element_type=jnp.float32) - 1.0
    slots = lax.broadcasted_iota(jnp.int32, (CAP, tokens), 0).astype(jnp.float32)
    lanes = lax.broadcasted_iota(jnp.int32, (tokens, CAP), 1).astype(jnp.float32)
    member_t, rank_t = member.T, rank.T
    for n, k in enumerate((BACK_HERE, BACK_LEFT, LEFT_HERE, LEFT_ON)):
        hit = (slots == rank[k : k + 1, :]) & (member[k : k + 1, :] > 0)
        place[n * CAP : (n + 1) * CAP, :] = hit.astype(jnp.bfloat16)
    for k in range(len(ask)):
        hit = (lanes == rank_t[:, k : k + 1]) & (member_t[:, k : k + 1] > 0)
        place_t[k * tokens : (k + 1) * tokens, :] = hit.astype(jnp.bfloat16)
    weight = [
        jnp.where(first, table[2:3, :], 0.0) + jnp.where(second, table[3:4, :], 0.0)
        for (table, _), (first, second) in zip(ask, names)
    ]
    weight_t[...] = jnp.concatenate(weight + [jnp.zeros_like(weight[0])] * (8 - len(weight)), axis=0).T


def routing(own, near, side):
    tokens = own.shape[1]
    outs = [like((len(PACKED) * CAP, tokens)), like((7 * tokens, CAP)), like((tokens, 8), jnp.float32)]
    return call(routing_body, outs, (own, near, side))


def packed(place, k, rows):
    hit = place[k * CAP : (k + 1) * CAP, :]
    return jnp.dot(hit, rows[...], preferred_element_type=jnp.float32).astype(jnp.bfloat16)


def pack_body(k, rows, place, after, out):
    out[...] = packed(place, k, rows)


def pack(k, rows, place, after):
    return call(functools.partial(pack_body, k), [like((CAP, rows.shape[1]))], (rows, place, after))[0]


def expert(rows, gain, wgate, wup, wdown):
    xf = rows.astype(jnp.float32)
    scale = lax.rsqrt(jnp.mean(xf * xf, axis=1, keepdims=True) + 1e-06)
    x = (xf * scale * gain[...]).astype(jnp.bfloat16)
    gpart = jnp.dot(x, wgate[...], preferred_element_type=jnp.float32)
    upart = jnp.dot(x, wup[...], preferred_element_type=jnp.float32)
    hidden = (gpart * jax.nn.sigmoid(gpart) * upart).astype(jnp.bfloat16)
    return jnp.dot(hidden, wdown[...], preferred_element_type=jnp.float32).astype(jnp.bfloat16)


def slots_body(rows, gain, wgate, wup, wdown, after, left, right):
    part = expert(rows[...], gain, wgate, wup, wdown)
    left[...] = part[:, : left.shape[1]]
    right[...] = part[:, left.shape[1] :]


def slots(rows, gain, weights, after, cut):
    outs = [like((CAP, cut)), like((CAP, weights[2].shape[1] - cut))]
    return call(slots_body, outs, (rows, gain, *weights, after), flops=6 * CAP * weights[0].size)


def side_body(rows, gain, wgate, wup, wdown, near_out, after, left, right, keep):
    part = expert(rows[...], gain, wgate, wup, wdown)
    half = left.shape[1]
    odd = lax.rem(lax.axis_index("section"), 2) == 1
    left[...] = part[:, :half]
    right[...] = jnp.where(odd, part[:, half:], near_out[:, half:])
    keep[...] = jnp.where(odd, near_out[:, half:], part[:, half:])


def sided(rows, gain, weights, near_out, after, cut):
    rest = like((CAP, weights[2].shape[1] - cut))
    outs = [like((CAP, cut)), rest, rest]
    return call(side_body, outs, (rows, gain, *weights, near_out, after), flops=6 * CAP * weights[0].size)


def tokens_body(k, rows, place, gain, wgate, wup, wdown, after, out):
    out[...] = expert(packed(place, k, rows), gain, wgate, wup, wdown)


def tokens(k, rows, place, gain, weights, after):
    outs = [like((CAP, weights[2].shape[1]))]
    ins = (rows, place, gain, *weights, after)
    return call(functools.partial(tokens_body, k), outs, ins, flops=6 * CAP * weights[0].size)[0]


STRIP = 256


def spread_body(which, first, carried, place_t, weight_t, *refs):
    parts, (out, *copies) = refs[:2], refs[2 + carried + 1 :]
    size, width = weight_t.shape[0], out.shape[1]
    for at in range(0, width, STRIP):
        terms = []
        for k, part in zip(which, parts):
            hit = place_t[k * size : (k + 1) * size, :]
            begin = at if part.shape[1] == width else first + at
            rows = jnp.dot(hit, part[:, begin : begin + STRIP], preferred_element_type=jnp.float32)
            terms.append(weight_t[:, k : k + 1] * rows)
        out[:, at : at + STRIP] = (terms[0] + terms[1]).astype(out.dtype)
    for value, copy in zip(refs[2 : 2 + carried], copies):
        copy[...] = value[...]


def spread(which, place_t, weight_t, parts, columns, after, carried=()):
    outs = [like((weight_t.shape[0], columns.stop - columns.start))] + [like(v.shape) for v in carried]
    body = functools.partial(spread_body, which, columns.start, len(carried))
    return call(body, outs, (place_t, weight_t, *parts, *carried, after))


def again_body(value, after, out):
    out[...] = value[...]


def again(value, after):
    return call(again_body, [like(value.shape)], (value, after))[0]


def based_body(rows, place_t, weight_t, here, left, out):
    half, size = left.shape[1], weight_t.shape[0]
    for at in range(0, out.shape[1], STRIP):
        strip = slice(at, at + STRIP)
        total = rows[:, strip].astype(jnp.float32)
        for k, part in ((BACK_HERE, here), (BACK_LEFT, left)):
            if at < half or k == BACK_HERE:
                hit = place_t[k * size : (k + 1) * size, :]
                slots_here = jnp.dot(hit, part[:, strip], preferred_element_type=jnp.float32)
                total = total + weight_t[:, k : k + 1] * slots_here
        out[:, strip] = total


def based(rows, place_t, weight_t, here, left):
    return call(based_body, [like(rows.shape, jnp.float32)], (rows, place_t, weight_t, here, left), flops=LONG)[0]


def written(value, here, out, first, done, n):
    width = value.shape[1]
    here[:, first : first + width] = value.astype(out.dtype)
    copy = pltpu.make_async_copy(here.at[:, pl.ds(first, width)], out.at[:, pl.ds(first, width)], done.at[n])
    copy.start()
    return copy


def first_body(base, left, out, rest, here, done):
    cut = left.shape[1]
    copies = []
    for n, at in enumerate(range(0, cut, STRIP)):
        strip = slice(at, at + STRIP)
        copies.append(written(base[:, strip] + left[:, strip].astype(jnp.float32), here, out, at, done, n))
    rest[...] = base[:, cut:]
    for copy in copies:
        copy.wait()


def rest_body(_, rest, place_t, weight_t, slots_right, right, out, here, done):
    cut, size = out.shape[1] - rest.shape[1], weight_t.shape[0]
    hit = place_t[BACK_RIGHT * size : (BACK_RIGHT + 1) * size, :]
    weight = weight_t[:, BACK_RIGHT : BACK_RIGHT + 1]
    copies = []
    for n, at in enumerate(range(0, rest.shape[1], STRIP)):
        strip = slice(at, at + STRIP)
        rows = jnp.dot(hit, slots_right[:, strip], preferred_element_type=jnp.float32)
        total = rest[:, strip] + weight * rows + right[:, strip].astype(jnp.float32)
        copies.append(written(total, here, out, cut + at, done, n))
    for copy in copies:
        copy.wait()


def last(base, place_t, weight_t, slots_right, left, right, dtype):
    out = like(base.shape, dtype)
    rest = like(right.shape, jnp.float32)
    common = dict(
        scratch_shapes=[VMEM(out.shape, dtype), pltpu.SemaphoreType.DMA((base.shape[1] // STRIP,))],
        compiler_params=pltpu.CompilerParams(vmem_limit_bytes=8 << 20),
        cost_estimate=pl.CostEstimate(flops=0, bytes_accessed=0, transcendentals=0),
    )
    result, rest = pl.pallas_call(
        first_body,
        out_shape=[out, rest],
        in_specs=[spec()] * 2,
        out_specs=[spec(pltpu.HBM), spec()],
        **common,
    )(base, left)
    return pl.pallas_call(
        rest_body,
        out_shape=out,
        in_specs=[spec(pltpu.HBM)] + [spec()] * 5,
        out_specs=spec(pltpu.HBM),
        input_output_aliases={0: 0},
        **common,
    )(result, rest, place_t, weight_t, slots_right, right)


def moved(value, back, flip):
    sections, experts = lax.axis_size("section"), lax.axis_size("expert")
    pairs = [
        ((s - back) % sections * experts + (e ^ flip(s)), s * experts + e)
        for s in range(sections)
        for e in range(experts)
    ]
    return lax.ppermute(value, ("section", "expert"), pairs)


def near_flip(section):
    return flips(section)[0]


def side_flip(section):
    return flips(section)[1]


LONG = 20_000_000_000
CUT = 5


def local_square(acts, routes, gates, norm_gain, gate_w, up_w, down_w):
    weights = (gate_w[0], up_w[0], down_w[0])
    near_rows = moved(acts[0], 1, near_flip)
    rows = moved(acts[0], 1, lambda s: 0)
    table, gain = tabled(routes[0].T, gates[0].T, norm_gain)
    near_table = moved(table, 0, near_flip)
    side_table = moved(table, 0, side_flip)
    place, place_t, weight_t = routing(table, near_table, side_table)
    onward = pack(NEAR_SIDE, near_rows, place, near_rows)
    far_rows = moved(onward, 0, side_flip)
    near_out = tokens(NEAR_HERE, near_rows, place, gain, weights, onward)
    side_send = pack(OWN_SIDE, rows, place, near_out)
    side_rows = moved(side_send, 0, side_flip)
    width = acts.shape[2]
    cut = width * CUT // 8
    far_left, far_right = slots(far_rows, gain, weights, side_send, cut)
    on_left = moved(far_left, 0, side_flip)
    on_right = moved(far_right, 0, lambda s: side_flip(s) if s % 2 else near_flip(s))
    left_slots, right_slots, keep = sided(side_rows, gain, weights, near_out, far_left, cut)
    left_slots = moved(left_slots, 0, side_flip)
    sums = functools.partial(spread, place_t=place_t, weight_t=weight_t)
    (left,) = sums((LEFT_HERE, LEFT_ON), parts=(near_out, on_left), columns=slice(0, cut), after=keep)
    (right,) = sums((RIGHT_HERE, RIGHT_ON), parts=(keep, on_right), columns=slice(cut, width), after=left)
    right_slots = again(right_slots, right)
    right_slots = moved(right_slots, 0, lambda s: side_flip(s) if s % 2 else near_flip(s))
    from_left = moved(left, 0, near_flip)
    from_right = moved(right, 0, lambda s: near_flip(s) if s % 2 else side_flip(s))
    here = tokens(OWN_HERE, rows, place, gain, weights, right)
    base = based(rows, place_t, weight_t, here, left_slots)
    return last(base, place_t, weight_t, right_slots, from_left, from_right, acts.dtype)[None]


def solution(mesh):
    in_specs = (
        P("section", "expert", None),
        P("section", "expert", None),
        P("section", "expert", None),
        P("section", None),
        P("section", None, "expert"),
        P("section", None, "expert"),
        P("section", "expert", None),
    )
    out_specs = P("section", "expert", None)
    local = local_square if mesh.shape["expert"] == NEXP else local_any
    return jax.shard_map(local, mesh=mesh, in_specs=in_specs, out_specs=out_specs, check_vma=False)
```

```python
import functools

import jax
import jax.numpy as jnp
from jax import lax
from jax.experimental import pallas as pl
from jax.experimental.pallas import tpu as pltpu
from jax.sharding import PartitionSpec as P

NEXP = 4
CAP = 96
VMEM = pltpu.VMEM


def shifted(value, axis, steps):
    count = lax.axis_size(axis)
    pairs = [(source, (source + steps) % count) for source in range(count)]
    return lax.ppermute(value, axis, pairs)


def expert_rows(rows, wgate, wup, wdown):
    gpart = jnp.einsum("scd,dh->sch", rows, wgate, preferred_element_type=jnp.float32)
    upart = jnp.einsum("scd,dh->sch", rows, wup, preferred_element_type=jnp.float32)
    hidden = (jax.nn.silu(gpart) * upart).astype(jnp.bfloat16)
    return jnp.einsum("sch,hd->scd", hidden, wdown, preferred_element_type=jnp.float32).astype(
        jnp.bfloat16
    )


def local_any(acts, routes, gates, norm_gain, gate_w, up_w, down_w):
    arrived = shifted(acts, "section", 1)[0]
    ids = routes[0]
    weights = gates[0]
    gain = norm_gain[0]
    wgate = gate_w[0]
    wup = up_w[0]
    wdown = down_w[0]
    hsplit = lax.axis_size("expert") // NEXP
    tok_count = ids.shape[0]
    chosen = (ids[:, :, None] == jnp.arange(NEXP, dtype=jnp.int32)[None, None, :]).astype(jnp.int32)
    member = jnp.sum(chosen, axis=1)
    gate_of = jnp.sum(weights[:, :, None] * chosen.astype(jnp.float32), axis=1)
    slot_rank = jnp.cumsum(member, axis=0) - 1
    slots = jnp.arange(CAP, dtype=jnp.int32)
    place = (slot_rank.T[:, None, :] == slots[None, :, None]) & (member.T[:, None, :] > 0)
    place_bf = place.astype(jnp.bfloat16)
    xf = arrived.astype(jnp.float32)
    scale = lax.rsqrt(jnp.mean(xf * xf, axis=1, keepdims=True) + 1e-06)
    normed = (xf * scale * gain[None, :]).astype(jnp.bfloat16)
    packed = jnp.einsum("gct,td->gcd", place_bf, normed, preferred_element_type=jnp.float32).astype(
        jnp.bfloat16
    )
    outgoing = jnp.repeat(packed, hsplit, axis=0)
    received = lax.all_to_all(outgoing, "expert", split_axis=0, concat_axis=0, tiled=True)
    returned = lax.all_to_all(
        expert_rows(received, wgate, wup, wdown), "expert", split_axis=0, concat_axis=0, tiled=True
    )
    shards = returned.reshape(NEXP, hsplit, CAP, returned.shape[-1])
    per_expert = jnp.einsum("gct,ghcd->gtd", place_bf, shards, preferred_element_type=jnp.float32)
    contrib = jnp.sum(per_expert * gate_of.T[:, :, None], axis=0)
    result = (xf + contrib).astype(jnp.bfloat16)
    return result.reshape(1, tok_count, result.shape[-1])


def spec(space=VMEM):
    return pl.BlockSpec(memory_space=space)


def call(body, outs, ins, limit=16, flops=0, scratch=()):
    return pl.pallas_call(
        body,
        out_shape=outs,
        in_specs=[spec()] * len(ins),
        out_specs=[spec() for _ in outs],
        scratch_shapes=scratch,
        compiler_params=pltpu.CompilerParams(vmem_limit_bytes=limit << 20),
        cost_estimate=pl.CostEstimate(flops=flops, bytes_accessed=0, transcendentals=0),
    )(*ins)


def like(shape, dtype=jnp.bfloat16):
    return jax.ShapeDtypeStruct(shape, dtype)


def flips(section):
    odd = section % 2
    return 1 + odd, 2 - odd


def position():
    me = lax.axis_index("expert")
    return me, me ^ (2 - lax.rem(lax.axis_index("section"), 2))


def table_body(ids, gates, gain, table, gain_out, ids_here, gates_here, done):
    copies = [(ids, ids_here), (gates, gates_here), (gain, gain_out)]
    copies = [pltpu.make_async_copy(source, target, done.at[n]) for n, (source, target) in enumerate(copies)]
    for copy in copies:
        copy.start()
    for copy in copies:
        copy.wait()
    table[0:2, :] = ids_here[...].astype(jnp.float32)
    table[2:4, :] = gates_here[...]
    table[4:8, :] = jnp.zeros((4, table.shape[1]), jnp.float32)


def tabled(ids, gates, gain):
    ins = [pltpu.with_memory_space_constraint(v, pltpu.HBM) for v in (ids, gates, gain)]
    return pl.pallas_call(
        table_body,
        out_shape=[like((8, ids.shape[1]), jnp.float32), like(gain.shape, gain.dtype)],
        in_specs=[spec(pltpu.HBM)] * 3,
        out_specs=[spec()] * 2,
        scratch_shapes=[VMEM(ids.shape, ids.dtype), VMEM(gates.shape, gates.dtype), pltpu.SemaphoreType.DMA((3,))],
        compiler_params=pltpu.CompilerParams(vmem_limit_bytes=4 << 20),
        cost_estimate=pl.CostEstimate(flops=LONG, bytes_accessed=0, transcendentals=0),
    )(*ins)


PACKED = OWN_HERE, OWN_SIDE, NEAR_HERE, NEAR_SIDE = range(4)
BACK_HERE, BACK_LEFT, BACK_RIGHT, LEFT_HERE, LEFT_ON, RIGHT_HERE, RIGHT_ON = range(7)


def routing_body(own, near, beside, place, place_t, weight_t):
    me, side = position()
    odd = lax.rem(lax.axis_index("section"), 2)
    other = side ^ (3 - 3 * odd)
    third = jnp.where(odd == 1, near[...], beside[...])
    own, near = own[...], near[...]
    ask = [(own, me), (own, side), (own, other), (near, me), (near, side), (third, me), (third, other)]
    names = [(table[0:1, :] == g.astype(jnp.float32), table[1:2, :] == g.astype(jnp.float32)) for table, g in ask]
    rows = [(first | second).astype(jnp.float32) for first, second in names]
    member = jnp.concatenate(rows + [jnp.zeros_like(rows[0])] * (8 - len(rows)), axis=0)
    tokens = member.shape[1]
    before = lax.broadcasted_iota(jnp.int32, (tokens, tokens), 0)
    at = lax.broadcasted_iota(jnp.int32, (tokens, tokens), 1)
    upto = (before <= at).astype(jnp.bfloat16)
    rank = jnp.dot(member.astype(jnp.bfloat16), upto, preferred_element_type=jnp.float32) - 1.0
    slots = lax.broadcasted_iota(jnp.int32, (CAP, tokens), 0).astype(jnp.float32)
    lanes = lax.broadcasted_iota(jnp.int32, (tokens, CAP), 1).astype(jnp.float32)
    member_t, rank_t = member.T, rank.T
    for n, k in enumerate((BACK_HERE, BACK_LEFT, LEFT_HERE, LEFT_ON)):
        hit = (slots == rank[k : k + 1, :]) & (member[k : k + 1, :] > 0)
        place[n * CAP : (n + 1) * CAP, :] = hit.astype(jnp.bfloat16)
    for k in range(len(ask)):
        hit = (lanes == rank_t[:, k : k + 1]) & (member_t[:, k : k + 1] > 0)
        place_t[k * tokens : (k + 1) * tokens, :] = hit.astype(jnp.bfloat16)
    weight = [
        jnp.where(first, table[2:3, :], 0.0) + jnp.where(second, table[3:4, :], 0.0)
        for (table, _), (first, second) in zip(ask, names)
    ]
    weight_t[...] = jnp.concatenate(weight + [jnp.zeros_like(weight[0])] * (8 - len(weight)), axis=0).T


def routing(own, near, side):
    tokens = own.shape[1]
    outs = [like((len(PACKED) * CAP, tokens)), like((7 * tokens, CAP)), like((tokens, 8), jnp.float32)]
    return call(routing_body, outs, (own, near, side))


def packed(place, k, rows):
    hit = place[k * CAP : (k + 1) * CAP, :]
    return jnp.dot(hit, rows[...], preferred_element_type=jnp.float32).astype(jnp.bfloat16)


def pack_body(k, rows, place, after, out):
    out[...] = packed(place, k, rows)


def pack(k, rows, place, after):
    return call(functools.partial(pack_body, k), [like((CAP, rows.shape[1]))], (rows, place, after))[0]


def expert(rows, gain, wgate, wup, wdown):
    xf = rows.astype(jnp.float32)
    scale = lax.rsqrt(jnp.mean(xf * xf, axis=1, keepdims=True) + 1e-06)
    x = (xf * scale * gain[...]).astype(jnp.bfloat16)
    gpart = jnp.dot(x, wgate[...], preferred_element_type=jnp.float32)
    upart = jnp.dot(x, wup[...], preferred_element_type=jnp.float32)
    hidden = (gpart * jax.nn.sigmoid(gpart) * upart).astype(jnp.bfloat16)
    return jnp.dot(hidden, wdown[...], preferred_element_type=jnp.float32).astype(jnp.bfloat16)


def slots_body(rows, gain, wgate, wup, wdown, after, left, right):
    part = expert(rows[...], gain, wgate, wup, wdown)
    left[...] = part[:, : left.shape[1]]
    right[...] = part[:, left.shape[1] :]


def slots(rows, gain, weights, after, cut):
    outs = [like((CAP, cut)), like((CAP, weights[2].shape[1] - cut))]
    return call(slots_body, outs, (rows, gain, *weights, after), flops=6 * CAP * weights[0].size)


def side_body(rows, gain, wgate, wup, wdown, near_out, after, left, right, keep):
    part = expert(rows[...], gain, wgate, wup, wdown)
    half = left.shape[1]
    odd = lax.rem(lax.axis_index("section"), 2) == 1
    left[...] = part[:, :half]
    right[...] = jnp.where(odd, part[:, half:], near_out[:, half:])
    keep[...] = jnp.where(odd, near_out[:, half:], part[:, half:])


def sided(rows, gain, weights, near_out, after, cut):
    rest = like((CAP, weights[2].shape[1] - cut))
    outs = [like((CAP, cut)), rest, rest]
    return call(side_body, outs, (rows, gain, *weights, near_out, after), flops=6 * CAP * weights[0].size)


def tokens_body(k, rows, place, gain, wgate, wup, wdown, after, out):
    out[...] = expert(packed(place, k, rows), gain, wgate, wup, wdown)


def tokens(k, rows, place, gain, weights, after):
    outs = [like((CAP, weights[2].shape[1]))]
    ins = (rows, place, gain, *weights, after)
    return call(functools.partial(tokens_body, k), outs, ins, flops=6 * CAP * weights[0].size)[0]


STRIP = 256


def spread_body(which, first, carried, place_t, weight_t, *refs):
    parts, (out, *copies) = refs[:2], refs[2 + carried + 1 :]
    size, width = weight_t.shape[0], out.shape[1]
    for at in range(0, width, STRIP):
        terms = []
        for k, part in zip(which, parts):
            hit = place_t[k * size : (k + 1) * size, :]
            begin = at if part.shape[1] == width else first + at
            rows = jnp.dot(hit, part[:, begin : begin + STRIP], preferred_element_type=jnp.float32)
            terms.append(weight_t[:, k : k + 1] * rows)
        out[:, at : at + STRIP] = (terms[0] + terms[1]).astype(out.dtype)
    for value, copy in zip(refs[2 : 2 + carried], copies):
        copy[...] = value[...]


def spread(which, place_t, weight_t, parts, columns, after, carried=()):
    outs = [like((weight_t.shape[0], columns.stop - columns.start))] + [like(v.shape) for v in carried]
    body = functools.partial(spread_body, which, columns.start, len(carried))
    return call(body, outs, (place_t, weight_t, *parts, *carried, after))


def again_body(value, after, out):
    out[...] = value[...]


def again(value, after):
    return call(again_body, [like(value.shape)], (value, after))[0]


def based_body(rows, place_t, weight_t, here, left, out):
    half, size = left.shape[1], weight_t.shape[0]
    for at in range(0, out.shape[1], STRIP):
        strip = slice(at, at + STRIP)
        total = rows[:, strip].astype(jnp.float32)
        for k, part in ((BACK_HERE, here), (BACK_LEFT, left)):
            if at < half or k == BACK_HERE:
                hit = place_t[k * size : (k + 1) * size, :]
                slots_here = jnp.dot(hit, part[:, strip], preferred_element_type=jnp.float32)
                total = total + weight_t[:, k : k + 1] * slots_here
        out[:, strip] = total


def based(rows, place_t, weight_t, here, left):
    return call(based_body, [like(rows.shape, jnp.float32)], (rows, place_t, weight_t, here, left), flops=LONG)[0]


def written(value, here, out, first, done, n):
    width = value.shape[1]
    here[:, first : first + width] = value.astype(out.dtype)
    copy = pltpu.make_async_copy(here.at[:, pl.ds(first, width)], out.at[:, pl.ds(first, width)], done.at[n])
    copy.start()
    return copy


def first_body(base, left, out, rest, here, done):
    cut = left.shape[1]
    copies = []
    for n, at in enumerate(range(0, cut, STRIP)):
        strip = slice(at, at + STRIP)
        copies.append(written(base[:, strip] + left[:, strip].astype(jnp.float32), here, out, at, done, n))
    rest[...] = base[:, cut:]
    for copy in copies:
        copy.wait()


def rest_body(_, rest, place_t, weight_t, slots_right, right, out, here, done):
    cut, size = out.shape[1] - rest.shape[1], weight_t.shape[0]
    hit = place_t[BACK_RIGHT * size : (BACK_RIGHT + 1) * size, :]
    weight = weight_t[:, BACK_RIGHT : BACK_RIGHT + 1]
    copies = []
    for n, at in enumerate(range(0, rest.shape[1], STRIP)):
        strip = slice(at, at + STRIP)
        rows = jnp.dot(hit, slots_right[:, strip], preferred_element_type=jnp.float32)
        total = rest[:, strip] + weight * rows + right[:, strip].astype(jnp.float32)
        copies.append(written(total, here, out, cut + at, done, n))
    for copy in copies:
        copy.wait()


def last(base, place_t, weight_t, slots_right, left, right, dtype):
    out = like(base.shape, dtype)
    rest = like(right.shape, jnp.float32)
    common = dict(
        scratch_shapes=[VMEM(out.shape, dtype), pltpu.SemaphoreType.DMA((base.shape[1] // STRIP,))],
        compiler_params=pltpu.CompilerParams(vmem_limit_bytes=8 << 20),
        cost_estimate=pl.CostEstimate(flops=0, bytes_accessed=0, transcendentals=0),
    )
    result, rest = pl.pallas_call(
        first_body,
        out_shape=[out, rest],
        in_specs=[spec()] * 2,
        out_specs=[spec(pltpu.HBM), spec()],
        **common,
    )(base, left)
    return pl.pallas_call(
        rest_body,
        out_shape=out,
        in_specs=[spec(pltpu.HBM)] + [spec()] * 5,
        out_specs=spec(pltpu.HBM),
        input_output_aliases={0: 0},
        **common,
    )(result, rest, place_t, weight_t, slots_right, right)


def moved(value, back, flip):
    sections, experts = lax.axis_size("section"), lax.axis_size("expert")
    pairs = [
        ((s - back) % sections * experts + (e ^ flip(s)), s * experts + e)
        for s in range(sections)
        for e in range(experts)
    ]
    return lax.ppermute(value, ("section", "expert"), pairs)


def near_flip(section):
    return flips(section)[0]


def side_flip(section):
    return flips(section)[1]


LONG = 20_000_000_000
CUT = 4


def local_square(acts, routes, gates, norm_gain, gate_w, up_w, down_w):
    weights = (gate_w[0], up_w[0], down_w[0])
    near_rows = moved(acts[0], 1, near_flip)
    rows = moved(acts[0], 1, lambda s: 0)
    table, gain = tabled(routes[0].T, gates[0].T, norm_gain)
    near_table = moved(table, 0, near_flip)
    side_table = moved(table, 0, side_flip)
    place, place_t, weight_t = routing(table, near_table, side_table)
    onward = pack(NEAR_SIDE, near_rows, place, near_rows)
    far_rows = moved(onward, 0, side_flip)
    near_out = tokens(NEAR_HERE, near_rows, place, gain, weights, onward)
    side_send = pack(OWN_SIDE, rows, place, near_out)
    side_rows = moved(side_send, 0, side_flip)
    width = acts.shape[2]
    cut = width * CUT // 8
    far_left, far_right = slots(far_rows, gain, weights, side_send, cut)
    on_left = moved(far_left, 0, side_flip)
    on_right = moved(far_right, 0, lambda s: side_flip(s) if s % 2 else near_flip(s))
    left_slots, right_slots, keep = sided(side_rows, gain, weights, near_out, far_left, cut)
    left_slots = moved(left_slots, 0, side_flip)
    sums = functools.partial(spread, place_t=place_t, weight_t=weight_t)
    (left,) = sums((LEFT_HERE, LEFT_ON), parts=(near_out, on_left), columns=slice(0, cut), after=keep)
    (right,) = sums((RIGHT_HERE, RIGHT_ON), parts=(keep, on_right), columns=slice(cut, width), after=left)
    right_slots = again(right_slots, right)
    right_slots = moved(right_slots, 0, lambda s: side_flip(s) if s % 2 else near_flip(s))
    from_left = moved(left, 0, near_flip)
    from_right = moved(right, 0, lambda s: near_flip(s) if s % 2 else side_flip(s))
    here = tokens(OWN_HERE, rows, place, gain, weights, right)
    base = based(rows, place_t, weight_t, here, left_slots)
    return last(base, place_t, weight_t, right_slots, from_left, from_right, acts.dtype)[None]


def solution(mesh):
    in_specs = (
        P("section", "expert", None),
        P("section", "expert", None),
        P("section", "expert", None),
        P("section", None),
        P("section", None, "expert"),
        P("section", None, "expert"),
        P("section", "expert", None),
    )
    out_specs = P("section", "expert", None)
    local = local_square if mesh.shape["expert"] == NEXP else local_any
    return jax.shard_map(local, mesh=mesh, in_specs=in_specs, out_specs=out_specs, check_vma=False)
```

```python
import functools

import jax
import jax.numpy as jnp
from jax import lax
from jax.experimental import pallas as pl
from jax.experimental.pallas import tpu as pltpu
from jax.sharding import PartitionSpec as P

NEXP = 4
CAP = 96
VMEM = pltpu.VMEM


def shifted(value, axis, steps):
    count = lax.axis_size(axis)
    pairs = [(source, (source + steps) % count) for source in range(count)]
    return lax.ppermute(value, axis, pairs)


def expert_rows(rows, wgate, wup, wdown):
    gpart = jnp.einsum("scd,dh->sch", rows, wgate, preferred_element_type=jnp.float32)
    upart = jnp.einsum("scd,dh->sch", rows, wup, preferred_element_type=jnp.float32)
    hidden = (jax.nn.silu(gpart) * upart).astype(jnp.bfloat16)
    return jnp.einsum("sch,hd->scd", hidden, wdown, preferred_element_type=jnp.float32).astype(
        jnp.bfloat16
    )


def local_any(acts, routes, gates, norm_gain, gate_w, up_w, down_w):
    arrived = shifted(acts, "section", 1)[0]
    ids = routes[0]
    weights = gates[0]
    gain = norm_gain[0]
    wgate = gate_w[0]
    wup = up_w[0]
    wdown = down_w[0]
    hsplit = lax.axis_size("expert") // NEXP
    tok_count = ids.shape[0]
    chosen = (ids[:, :, None] == jnp.arange(NEXP, dtype=jnp.int32)[None, None, :]).astype(jnp.int32)
    member = jnp.sum(chosen, axis=1)
    gate_of = jnp.sum(weights[:, :, None] * chosen.astype(jnp.float32), axis=1)
    slot_rank = jnp.cumsum(member, axis=0) - 1
    slots = jnp.arange(CAP, dtype=jnp.int32)
    place = (slot_rank.T[:, None, :] == slots[None, :, None]) & (member.T[:, None, :] > 0)
    place_bf = place.astype(jnp.bfloat16)
    xf = arrived.astype(jnp.float32)
    scale = lax.rsqrt(jnp.mean(xf * xf, axis=1, keepdims=True) + 1e-06)
    normed = (xf * scale * gain[None, :]).astype(jnp.bfloat16)
    packed = jnp.einsum("gct,td->gcd", place_bf, normed, preferred_element_type=jnp.float32).astype(
        jnp.bfloat16
    )
    outgoing = jnp.repeat(packed, hsplit, axis=0)
    received = lax.all_to_all(outgoing, "expert", split_axis=0, concat_axis=0, tiled=True)
    returned = lax.all_to_all(
        expert_rows(received, wgate, wup, wdown), "expert", split_axis=0, concat_axis=0, tiled=True
    )
    shards = returned.reshape(NEXP, hsplit, CAP, returned.shape[-1])
    per_expert = jnp.einsum("gct,ghcd->gtd", place_bf, shards, preferred_element_type=jnp.float32)
    contrib = jnp.sum(per_expert * gate_of.T[:, :, None], axis=0)
    result = (xf + contrib).astype(jnp.bfloat16)
    return result.reshape(1, tok_count, result.shape[-1])


def spec(space=VMEM):
    return pl.BlockSpec(memory_space=space)


def call(body, outs, ins, limit=16, flops=0, scratch=()):
    return pl.pallas_call(
        body,
        out_shape=outs,
        in_specs=[spec()] * len(ins),
        out_specs=[spec() for _ in outs],
        scratch_shapes=scratch,
        compiler_params=pltpu.CompilerParams(vmem_limit_bytes=limit << 20),
        cost_estimate=pl.CostEstimate(flops=flops, bytes_accessed=0, transcendentals=0),
    )(*ins)


def like(shape, dtype=jnp.bfloat16):
    return jax.ShapeDtypeStruct(shape, dtype)


def flips(section):
    odd = section % 2
    return 1 + odd, 2 - odd


def position():
    me = lax.axis_index("expert")
    return me, me ^ (2 - lax.rem(lax.axis_index("section"), 2))


def table_body(ids, gates, gain, table, gain_out, ids_here, gates_here, done):
    copies = [(ids, ids_here), (gates, gates_here), (gain, gain_out)]
    copies = [pltpu.make_async_copy(source, target, done.at[n]) for n, (source, target) in enumerate(copies)]
    for copy in copies:
        copy.start()
    for copy in copies:
        copy.wait()
    table[0:2, :] = ids_here[...].astype(jnp.float32)
    table[2:4, :] = gates_here[...]
    table[4:8, :] = jnp.zeros((4, table.shape[1]), jnp.float32)


def tabled(ids, gates, gain):
    ins = [pltpu.with_memory_space_constraint(v, pltpu.HBM) for v in (ids, gates, gain)]
    return pl.pallas_call(
        table_body,
        out_shape=[like((8, ids.shape[1]), jnp.float32), like(gain.shape, gain.dtype)],
        in_specs=[spec(pltpu.HBM)] * 3,
        out_specs=[spec()] * 2,
        scratch_shapes=[VMEM(ids.shape, ids.dtype), VMEM(gates.shape, gates.dtype), pltpu.SemaphoreType.DMA((3,))],
        compiler_params=pltpu.CompilerParams(vmem_limit_bytes=4 << 20),
        cost_estimate=pl.CostEstimate(flops=LONG, bytes_accessed=0, transcendentals=0),
    )(*ins)


PACKED = OWN_HERE, OWN_SIDE, NEAR_HERE, NEAR_SIDE = range(4)
BACK_HERE, BACK_LEFT, BACK_RIGHT, LEFT_HERE, LEFT_ON, RIGHT_HERE, RIGHT_ON = range(7)


def routing_body(own, near, beside, place, place_t, weight_t):
    me, side = position()
    odd = lax.rem(lax.axis_index("section"), 2)
    other = side ^ (3 - 3 * odd)
    third = jnp.where(odd == 1, near[...], beside[...])
    own, near = own[...], near[...]
    ask = [(own, me), (own, side), (own, other), (near, me), (near, side), (third, me), (third, other)]
    names = [(table[0:1, :] == g.astype(jnp.float32), table[1:2, :] == g.astype(jnp.float32)) for table, g in ask]
    rows = [(first | second).astype(jnp.float32) for first, second in names]
    member = jnp.concatenate(rows + [jnp.zeros_like(rows[0])] * (8 - len(rows)), axis=0)
    tokens = member.shape[1]
    before = lax.broadcasted_iota(jnp.int32, (tokens, tokens), 0)
    at = lax.broadcasted_iota(jnp.int32, (tokens, tokens), 1)
    upto = (before <= at).astype(jnp.bfloat16)
    rank = jnp.dot(member.astype(jnp.bfloat16), upto, preferred_element_type=jnp.float32) - 1.0
    slots = lax.broadcasted_iota(jnp.int32, (CAP, tokens), 0).astype(jnp.float32)
    lanes = lax.broadcasted_iota(jnp.int32, (tokens, CAP), 1).astype(jnp.float32)
    member_t, rank_t = member.T, rank.T
    for n, k in enumerate((BACK_HERE, BACK_LEFT, LEFT_HERE, LEFT_ON)):
        hit = (slots == rank[k : k + 1, :]) & (member[k : k + 1, :] > 0)
        place[n * CAP : (n + 1) * CAP, :] = hit.astype(jnp.bfloat16)
    for k in range(len(ask)):
        hit = (lanes == rank_t[:, k : k + 1]) & (member_t[:, k : k + 1] > 0)
        place_t[k * tokens : (k + 1) * tokens, :] = hit.astype(jnp.bfloat16)
    weight = [
        jnp.where(first, table[2:3, :], 0.0) + jnp.where(second, table[3:4, :], 0.0)
        for (table, _), (first, second) in zip(ask, names)
    ]
    weight_t[...] = jnp.concatenate(weight + [jnp.zeros_like(weight[0])] * (8 - len(weight)), axis=0).T


def routing(own, near, side):
    tokens = own.shape[1]
    outs = [like((len(PACKED) * CAP, tokens)), like((7 * tokens, CAP)), like((tokens, 8), jnp.float32)]
    return call(routing_body, outs, (own, near, side))


def packed(place, k, rows):
    hit = place[k * CAP : (k + 1) * CAP, :]
    return jnp.dot(hit, rows[...], preferred_element_type=jnp.float32).astype(jnp.bfloat16)


def pack_body(k, rows, place, after, out):
    out[...] = packed(place, k, rows)


def pack(k, rows, place, after):
    return call(functools.partial(pack_body, k), [like((CAP, rows.shape[1]))], (rows, place, after))[0]


def expert(rows, gain, wgate, wup, wdown):
    xf = rows.astype(jnp.float32)
    scale = lax.rsqrt(jnp.mean(xf * xf, axis=1, keepdims=True) + 1e-06)
    x = (xf * scale * gain[...]).astype(jnp.bfloat16)
    gpart = jnp.dot(x, wgate[...], preferred_element_type=jnp.float32)
    upart = jnp.dot(x, wup[...], preferred_element_type=jnp.float32)
    hidden = (gpart * jax.nn.sigmoid(gpart) * upart).astype(jnp.bfloat16)
    return jnp.dot(hidden, wdown[...], preferred_element_type=jnp.float32).astype(jnp.bfloat16)


def slots_body(rows, gain, wgate, wup, wdown, after, left, right):
    part = expert(rows[...], gain, wgate, wup, wdown)
    left[...] = part[:, : left.shape[1]]
    right[...] = part[:, left.shape[1] :]


def slots(rows, gain, weights, after, cut):
    outs = [like((CAP, cut)), like((CAP, weights[2].shape[1] - cut))]
    return call(slots_body, outs, (rows, gain, *weights, after), flops=6 * CAP * weights[0].size)


def side_body(rows, gain, wgate, wup, wdown, near_out, after, left, right, keep):
    part = expert(rows[...], gain, wgate, wup, wdown)
    half = left.shape[1]
    odd = lax.rem(lax.axis_index("section"), 2) == 1
    left[...] = part[:, :half]
    right[...] = jnp.where(odd, part[:, half:], near_out[:, half:])
    keep[...] = jnp.where(odd, near_out[:, half:], part[:, half:])


def sided(rows, gain, weights, near_out, after, cut):
    rest = like((CAP, weights[2].shape[1] - cut))
    outs = [like((CAP, cut)), rest, rest]
    return call(side_body, outs, (rows, gain, *weights, near_out, after), flops=6 * CAP * weights[0].size)


def tokens_body(k, rows, place, gain, wgate, wup, wdown, after, out):
    out[...] = expert(packed(place, k, rows), gain, wgate, wup, wdown)


def tokens(k, rows, place, gain, weights, after):
    outs = [like((CAP, weights[2].shape[1]))]
    ins = (rows, place, gain, *weights, after)
    return call(functools.partial(tokens_body, k), outs, ins, flops=6 * CAP * weights[0].size)[0]


STRIP = 256


def spread_body(which, first, carried, place_t, weight_t, *refs):
    parts, (out, *copies) = refs[:2], refs[2 + carried + 1 :]
    size, width = weight_t.shape[0], out.shape[1]
    for at in range(0, width, STRIP):
        terms = []
        for k, part in zip(which, parts):
            hit = place_t[k * size : (k + 1) * size, :]
            begin = at if part.shape[1] == width else first + at
            rows = jnp.dot(hit, part[:, begin : begin + STRIP], preferred_element_type=jnp.float32)
            terms.append(weight_t[:, k : k + 1] * rows)
        out[:, at : at + STRIP] = (terms[0] + terms[1]).astype(out.dtype)
    for value, copy in zip(refs[2 : 2 + carried], copies):
        copy[...] = value[...]


def spread(which, place_t, weight_t, parts, columns, after, carried=()):
    outs = [like((weight_t.shape[0], columns.stop - columns.start))] + [like(v.shape) for v in carried]
    body = functools.partial(spread_body, which, columns.start, len(carried))
    return call(body, outs, (place_t, weight_t, *parts, *carried, after))


def again_body(value, after, out):
    out[...] = value[...]


def again(value, after):
    return call(again_body, [like(value.shape)], (value, after))[0]


def based_body(rows, place_t, weight_t, here, left, out):
    half, size = left.shape[1], weight_t.shape[0]
    for at in range(0, out.shape[1], STRIP):
        strip = slice(at, at + STRIP)
        total = rows[:, strip].astype(jnp.float32)
        for k, part in ((BACK_HERE, here), (BACK_LEFT, left)):
            if at < half or k == BACK_HERE:
                hit = place_t[k * size : (k + 1) * size, :]
                slots_here = jnp.dot(hit, part[:, strip], preferred_element_type=jnp.float32)
                total = total + weight_t[:, k : k + 1] * slots_here
        out[:, strip] = total


def based(rows, place_t, weight_t, here, left):
    return call(based_body, [like(rows.shape, jnp.float32)], (rows, place_t, weight_t, here, left), flops=LONG)[0]


def written(value, here, out, first, done, n):
    width = value.shape[1]
    here[:, first : first + width] = value.astype(out.dtype)
    copy = pltpu.make_async_copy(here.at[:, pl.ds(first, width)], out.at[:, pl.ds(first, width)], done.at[n])
    copy.start()
    return copy


def first_body(base, left, out, here, done):
    cut = left.shape[1]
    copies = []
    for n, at in enumerate(range(0, cut, STRIP)):
        strip = slice(at, at + STRIP)
        copies.append(written(base[:, strip] + left[:, strip].astype(jnp.float32), here, out, at, done, n))
    for copy in copies:
        copy.wait()


def rest_body(_, base, place_t, weight_t, slots_right, right, out, here, done):
    cut, size = out.shape[1] - right.shape[1], weight_t.shape[0]
    hit = place_t[BACK_RIGHT * size : (BACK_RIGHT + 1) * size, :]
    weight = weight_t[:, BACK_RIGHT : BACK_RIGHT + 1]
    copies = []
    for n, at in enumerate(range(0, right.shape[1], STRIP)):
        strip = slice(at, at + STRIP)
        rows = jnp.dot(hit, slots_right[:, strip], preferred_element_type=jnp.float32)
        total = base[:, cut + at : cut + at + STRIP] + weight * rows + right[:, strip].astype(jnp.float32)
        copies.append(written(total, here, out, cut + at, done, n))
    for copy in copies:
        copy.wait()


def last(base, place_t, weight_t, slots_right, left, right, dtype):
    out = like(base.shape, dtype)
    common = dict(
        scratch_shapes=[VMEM(out.shape, dtype), pltpu.SemaphoreType.DMA((base.shape[1] // STRIP,))],
        compiler_params=pltpu.CompilerParams(vmem_limit_bytes=8 << 20),
        cost_estimate=pl.CostEstimate(flops=0, bytes_accessed=0, transcendentals=0),
    )
    result = pl.pallas_call(
        first_body,
        out_shape=out,
        in_specs=[spec()] * 2,
        out_specs=spec(pltpu.HBM),
        **common,
    )(base, left)
    return pl.pallas_call(
        rest_body,
        out_shape=out,
        in_specs=[spec(pltpu.HBM)] + [spec()] * 5,
        out_specs=spec(pltpu.HBM),
        input_output_aliases={0: 0},
        **common,
    )(result, base, place_t, weight_t, slots_right, right)


def moved(value, back, flip):
    sections, experts = lax.axis_size("section"), lax.axis_size("expert")
    pairs = [
        ((s - back) % sections * experts + (e ^ flip(s)), s * experts + e)
        for s in range(sections)
        for e in range(experts)
    ]
    return lax.ppermute(value, ("section", "expert"), pairs)


def near_flip(section):
    return flips(section)[0]


def side_flip(section):
    return flips(section)[1]


LONG = 20_000_000_000
CUT = 5


def local_square(acts, routes, gates, norm_gain, gate_w, up_w, down_w):
    weights = (gate_w[0], up_w[0], down_w[0])
    near_rows = moved(acts[0], 1, near_flip)
    rows = moved(acts[0], 1, lambda s: 0)
    table, gain = tabled(routes[0].T, gates[0].T, norm_gain)
    near_table = moved(table, 0, near_flip)
    side_table = moved(table, 0, side_flip)
    place, place_t, weight_t = routing(table, near_table, side_table)
    onward = pack(NEAR_SIDE, near_rows, place, near_rows)
    far_rows = moved(onward, 0, side_flip)
    near_out = tokens(NEAR_HERE, near_rows, place, gain, weights, onward)
    side_send = pack(OWN_SIDE, rows, place, near_out)
    side_rows = moved(side_send, 0, side_flip)
    width = acts.shape[2]
    cut = width * CUT // 8
    far_left, far_right = slots(far_rows, gain, weights, side_send, cut)
    on_left = moved(far_left, 0, side_flip)
    on_right = moved(far_right, 0, lambda s: side_flip(s) if s % 2 else near_flip(s))
    left_slots, right_slots, keep = sided(side_rows, gain, weights, near_out, far_left, cut)
    left_slots = moved(left_slots, 0, side_flip)
    sums = functools.partial(spread, place_t=place_t, weight_t=weight_t)
    (left,) = sums((LEFT_HERE, LEFT_ON), parts=(near_out, on_left), columns=slice(0, cut), after=keep)
    (right,) = sums((RIGHT_HERE, RIGHT_ON), parts=(keep, on_right), columns=slice(cut, width), after=left)
    right_slots = again(right_slots, right)
    right_slots = moved(right_slots, 0, lambda s: side_flip(s) if s % 2 else near_flip(s))
    from_left = moved(left, 0, near_flip)
    from_right = moved(right, 0, lambda s: near_flip(s) if s % 2 else side_flip(s))
    here = tokens(OWN_HERE, rows, place, gain, weights, right)
    base = based(rows, place_t, weight_t, here, left_slots)
    return last(base, place_t, weight_t, right_slots, from_left, from_right, acts.dtype)[None]


def solution(mesh):
    in_specs = (
        P("section", "expert", None),
        P("section", "expert", None),
        P("section", "expert", None),
        P("section", None),
        P("section", None, "expert"),
        P("section", None, "expert"),
        P("section", "expert", None),
    )
    out_specs = P("section", "expert", None)
    local = local_square if mesh.shape["expert"] == NEXP else local_any
    return jax.shard_map(local, mesh=mesh, in_specs=in_specs, out_specs=out_specs, check_vma=False)
```
